32 devices in a mesh: lsec: 4 (over z), rsec: 2 (over y), mpo: 4 (over x, core).
Axes of the slice: x: 2, y: 2, z: 4, core: 2. Of those that a mesh axis runs over, the one named last changes fastest.
Arguments:
- wavefunction: bfloat16 [64, 128, 128], P(('lsec', 'rsec')), may hold values from -6 to 6
- left_env: bfloat16 [40, 16, 128, 128], P('mpo', 'lsec'), may hold values from -0.5 to 0.5
- right_env: bfloat16 [40, 8, 128, 128], P('mpo', 'rsec'), may hold values from -0.125 to 0.125
- left_sizes: int32 [16], P('lsec'), may hold values from 64 to 128
- right_sizes: int32 [8], P('rsec'), may hold values from 64 to 128
- tile_left: int32 [64], P(('lsec', 'rsec')), may hold values from 0 to 3
- tile_right: int32 [64], P(('lsec', 'rsec')), may hold values from 0 to 3
- send_slot: int32 [40, 64], P('mpo', ('lsec', 'rsec')), may hold values from 0 to 8, as said below
- recv_tile: int32 [4, 64], P('mpo', ('lsec', 'rsec')), may hold values from 0 to 8, as said below
Outputs:
- hpsi: bfloat16 [64, 128, 128], P(('lsec', 'rsec', 'mpo'))
The draws below stay inside these ranges and needn't reach their ends.
Inputs may be any that keep to these rules, and one draw needn't show every extreme that they name: `send_slot`: the value 8 means that the MPO bond index has no block on the tile; any other value q is a device pair index l * (devices along rsec) + r. `recv_tile`: entry [m, q * 8 + s] is the tile on pair q into which pair s adds its slot for q under mpo index m, and 8 exactly where no entry of send_slot of pair s in group m names q.
All inputs are finite; a program needn't handle non-finite values.
Results may differ from the reference program's by a relative error of at most 0.0075.
Values may be sent and summed in bfloat16 or wider, within the bound.
No kernel may reach another device: no remote copies, remote signals or barrier semaphores. Data moves between devices by JAX's collectives and lax.ppermute only.
A program may use at most 64 MiB of HBM per device.

```python
import jax
import jax.numpy as jnp
from jax import lax

S = 128
A_DEV = 10
LS_DEV = 4
RS_DEV = 4
TILE_DEV = 8
MPO_DEVS = 4
PEERS = 8
W = 40
NL = 16
NR = 8
NTILES = 64
N_LSEC = 4
N_RSEC = 2
N_MPO = 4


def routing_tables(key):
    base_key = jax.random.fold_in(key, 7)
    key_level = jax.random.fold_in(base_key, 1)
    key_rolled = jax.random.fold_in(base_key, 2)
    key_peer = jax.random.fold_in(base_key, 3)
    key_target = jax.random.fold_in(base_key, 4)
    activity = jax.random.randint(key_level, (1, PEERS), 1, 5)
    activity_full = jnp.repeat(activity, TILE_DEV, axis=1)
    rolled = jax.random.randint(key_rolled, (W, NTILES), 0, 4)
    peer_of = jax.random.randint(key_peer, (W, NTILES), 0, PEERS)
    slot_of = jnp.where(rolled < activity_full, peer_of, PEERS)
    slot_of = slot_of.at[0, 0].set(0).at[W - 1, NTILES - 1].set(PEERS)
    target = jax.random.randint(key_target, (MPO_DEVS, PEERS, PEERS), 0, TILE_DEV)
    group_of = jnp.broadcast_to((jnp.arange(W) // A_DEV)[:, None], (W, NTILES))
    source_of = jnp.broadcast_to((jnp.arange(NTILES) // TILE_DEV)[None, :], (W, NTILES))
    sent_count = jnp.zeros((MPO_DEVS, PEERS, PEERS + 1), jnp.int32).at[group_of, source_of, slot_of].add(1)[:, :, :PEERS]
    receive = jnp.where(sent_count > 0, target, TILE_DEV)
    receive = jnp.transpose(receive, (0, 2, 1)).reshape(MPO_DEVS, PEERS * PEERS)
    return (slot_of.astype(jnp.int32), receive.astype(jnp.int32))


def draw_send_slot(key, part):
    return routing_tables(key)[0]


def draw_recv_tile(key, part):
    return routing_tables(key)[1]


def set_ends(entries, own_key, least, largest):
    longest = entries.shape.index(max(entries.shape))
    spots = []
    for shift in (0, 1):
        where = [jax.random.randint(jax.random.fold_in(own_key, axis), (), 0, length) for axis, length in enumerate(entries.shape)]
        where[longest] = (where[longest] + shift) % entries.shape[longest]
        spots.append(tuple(where))
    return entries.at[spots[0]].set(least).at[spots[1]].set(largest)


def levels(stream_key, dims, shards, low, high):
    level, own = 1.0, jax.random.fold_in(stream_key, 6)
    for dim, shards_of in shards:
        steps = jnp.exp(jax.random.uniform(jax.random.fold_in(own, dim), (shards_of,), jnp.float32, low / len(shards), high / len(shards)))
        level = level * jnp.repeat(steps, dims[dim] // shards_of).reshape([-1 if axis == dim else 1 for axis in range(len(dims))])
    return level


def scatter_about(stream_key, dims, scale, reach, cuts=(), kind=jnp.bfloat16):
    factor_of = levels(stream_key, dims, cuts, -0.22, 0.18) if cuts else 1.0
    values = jax.random.normal(stream_key, dims, jnp.float32) * scale * factor_of
    return jnp.minimum(jnp.maximum(values, -reach), reach).astype(kind)


def setup_inputs(seed: int = 0) -> dict:
    keys = jax.random.split(jax.random.key(seed), 10)
    return {
        "wavefunction": scatter_about(keys[0], (NTILES, S, S), 1.0, 6.0, ((0, 8),)),
        "left_env": scatter_about(keys[1], (W, NL, S, S), S ** -0.5, 0.5, ((0, 4), (1, 4))),
        "right_env": scatter_about(keys[2], (W, NR, S, S), (S * 16) ** -0.5, 0.125, ((0, 4), (1, 2))),
        "left_sizes": set_ends(jax.random.randint(keys[3], (NL,), S // 2, S + 1), jax.random.fold_in(keys[3], 1), S // 2, S).astype(jnp.int32),
        "right_sizes": set_ends(jax.random.randint(keys[4], (NR,), S // 2, S + 1), jax.random.fold_in(keys[4], 1), S // 2, S).astype(jnp.int32),
        "tile_left": set_ends(jax.random.randint(keys[5], (NTILES,), 0, LS_DEV), jax.random.fold_in(keys[5], 1), 0, LS_DEV - 1).astype(jnp.int32),
        "tile_right": set_ends(jax.random.randint(keys[6], (NTILES,), 0, RS_DEV), jax.random.fold_in(keys[6], 1), 0, RS_DEV - 1).astype(jnp.int32),
        "send_slot": draw_send_slot(jax.random.fold_in(keys[9], 71), 0),
        "recv_tile": draw_recv_tile(jax.random.fold_in(keys[9], 71), 0),
    }


def reference(wavefunction, left_env, right_env, left_sizes, right_sizes, tile_left, tile_right, send_slot, recv_tile):
    peer_count = N_LSEC * N_RSEC
    tile_total = TILE_DEV * peer_count
    owner_dev = jnp.arange(tile_total, dtype=jnp.int32) // TILE_DEV
    left_index = ((owner_dev // N_RSEC) * LS_DEV + tile_left).astype(jnp.int32)
    right_index = ((owner_dev % N_RSEC) * RS_DEV + tile_right).astype(jnp.int32)
    live_rows = left_sizes[left_index]
    live_cols = right_sizes[right_index]
    position = jnp.arange(S, dtype=jnp.int32)
    inside = (position[None, :, None] < live_rows[:, None, None]) & (position[None, None, :] < live_cols[:, None, None])
    masked = jnp.where(inside, wavefunction, jnp.zeros_like(wavefunction))
    total = jnp.zeros((tile_total, S, S), jnp.float32)
    peer_axis = jnp.arange(peer_count, dtype=jnp.int32)
    for mpo_at in range(N_MPO):
        left_group = left_env[mpo_at * A_DEV:(mpo_at + 1) * A_DEV]
        right_group = right_env[mpo_at * A_DEV:(mpo_at + 1) * A_DEV]
        slot_group = send_slot[mpo_at * A_DEV:(mpo_at + 1) * A_DEV]
        receive = recv_tile[mpo_at]

        def source_step(carry, source):
            begin_at = (source * TILE_DEV).astype(jnp.int32)
            source_tiles = lax.dynamic_slice_in_dim(masked, begin_at, TILE_DEV, 0).astype(jnp.float32)
            lidx = lax.dynamic_slice_in_dim(left_index, begin_at, TILE_DEV, 0)
            ridx = lax.dynamic_slice_in_dim(right_index, begin_at, TILE_DEV, 0)
            left_blocks = jnp.take(left_group, lidx, axis=1).astype(jnp.float32)
            right_blocks = jnp.take(right_group, ridx, axis=1).astype(jnp.float32)
            right_done = jnp.einsum("tpq,atrq->atpr", source_tiles, right_blocks).astype(jnp.bfloat16)
            right_done = lax.optimization_barrier(right_done).astype(jnp.float32)
            coupled = jnp.einsum("atop,atpr->ator", left_blocks, right_done)
            slot_ids = lax.dynamic_slice_in_dim(slot_group, begin_at, TILE_DEV, 1).reshape(-1)
            slots = jax.ops.segment_sum(coupled.reshape(-1, S, S), slot_ids, num_segments=peer_count + 1)[:peer_count]
            slots = lax.optimization_barrier(slots.astype(jnp.bfloat16)).astype(jnp.float32)
            target = receive[peer_axis * peer_count + source]
            destin = jnp.where(target < TILE_DEV, peer_axis * TILE_DEV + target, tile_total).astype(jnp.int32)
            return carry.at[destin].add(slots), None

        summed, _ = lax.scan(source_step, jnp.zeros((tile_total + 1, S, S), jnp.float32), jnp.arange(peer_count, dtype=jnp.int32))
        rounded = lax.optimization_barrier(summed[:tile_total].astype(jnp.bfloat16)).astype(jnp.float32)
        total = total + rounded
    return jnp.where(inside, total, jnp.zeros_like(total)).astype(jnp.bfloat16)
```

```python
import functools

import jax
import jax.numpy as jnp
from jax import lax
from jax.experimental import pallas as pl
from jax.experimental.pallas import tpu as pltpu
from jax.sharding import PartitionSpec as P

SMEM = pl.BlockSpec(memory_space=pltpu.SMEM)
VMEM = pl.BlockSpec(memory_space=pltpu.VMEM)
ANY = pl.BlockSpec(memory_space=pl.ANY)


def inside(states, rows, cols):
    at_row = lax.broadcasted_iota(jnp.int32, (states, states), 0)
    at_col = lax.broadcasted_iota(jnp.int32, (states, states), 1)
    return (at_row < rows) & (at_col < cols)


def couple_kernel(
    groups,
    tile_left,
    tile_right,
    left_sizes,
    right_sizes,
    send_slot,
    wave_hbm,
    left_hbm,
    right_hbm,
    *rest,
):
    outs = rest[: len(groups)]
    wave, left, right, masked, done, total, wave_sem, left_sem, right_sem = rest[len(groups) :]
    bonds, tiles, states = left.shape[0], wave.shape[0], wave.shape[1]
    wave_copy = pltpu.make_async_copy(wave_hbm, wave, wave_sem)
    wave_copy.start()

    def copies(a):
        return (
            pltpu.make_async_copy(right_hbm.at[a], right.at[a], right_sem.at[a]),
            pltpu.make_async_copy(left_hbm.at[a], left.at[a], left_sem.at[a]),
        )

    for a in range(bonds):
        for copy in copies(a):
            copy.start()
    total[...] = jnp.zeros_like(total)
    wave_copy.wait()
    for g in range(tiles):
        keep = inside(states, left_sizes[tile_left[g]], right_sizes[tile_right[g]])
        tile = wave[g].astype(jnp.float32)
        masked[g] = jnp.where(keep, tile, 0.0).astype(jnp.bfloat16)

    @pl.loop(0, bonds)
    def _(a):
        for copy in copies(a):
            copy.wait()
        for g in range(tiles):
            done[g] = lax.dot_general(
                masked[g],
                right[a, tile_right[g]],
                (((1,), (1,)), ((), ())),
                preferred_element_type=jnp.float32,
            ).astype(jnp.bfloat16)
        for g in range(tiles):
            q = send_slot[g, a]
            total[q] += jnp.dot(
                left[a, tile_left[g]], done[g], preferred_element_type=jnp.float32
            )

    for out, order in zip(outs, groups):
        for j, q in enumerate(order()):
            out[j] = total[q].astype(jnp.bfloat16)


def couple(groups, peers, tile_left, tile_right, left_sizes, right_sizes, send_slot, wave, left, right):
    tiles, states = wave.shape[0], wave.shape[1]
    bonds = left.shape[0]
    return pl.pallas_call(
        functools.partial(couple_kernel, [g for g, _ in groups]),
        out_shape=[
            jax.ShapeDtypeStruct((count, states, states), jnp.bfloat16) for _, count in groups
        ],
        in_specs=[SMEM] * 5 + [ANY] * 3,
        out_specs=[VMEM] * len(groups),
        scratch_shapes=[
            pltpu.VMEM(wave.shape, jnp.bfloat16),
            pltpu.VMEM(left.shape, jnp.bfloat16),
            pltpu.VMEM(right.shape, jnp.bfloat16),
            pltpu.VMEM(wave.shape, jnp.bfloat16),
            pltpu.VMEM(wave.shape, jnp.bfloat16),
            pltpu.VMEM((peers + 1, states, states), jnp.float32),
            pltpu.SemaphoreType.DMA,
            pltpu.SemaphoreType.DMA((bonds,)),
            pltpu.SemaphoreType.DMA((bonds,)),
        ],
        compiler_params=pltpu.CompilerParams(vmem_limit_bytes=40 * 1024 * 1024),
        name="couple",
    )(tile_left, tile_right, left_sizes, right_sizes, send_slot.T, wave, left, right)


def gather_kernel(n_left, own_table, other_table, *rest):
    received = rest[:n_left]
    give, keep, total = rest[n_left:]
    z, y = lax.axis_index("lsec"), lax.axis_index("rsec")
    c = lax.rem(lax.axis_index("mpo"), 2)
    total[...] = jnp.zeros_like(total)
    for k in range(n_left):
        source = 2 * jnp.bitwise_xor(z, k) + jnp.bitwise_xor(y, c)
        for j, table in enumerate((own_table, other_table)):
            t = table[0, source]
            total[t] += received[k][j].astype(jnp.float32)
    quarter = (total.shape[0] - 1) // 4
    for x in range(2):
        for j in range(quarter):
            give[x * quarter + j] = total[(2 * x + 1 - c) * quarter + j].astype(jnp.bfloat16)
            keep[x * quarter + j] = total[(2 * x + c) * quarter + j]


def gather(own_table, other_table, received, tiles):
    states = received[0].shape[1]
    return pl.pallas_call(
        functools.partial(gather_kernel, len(received)),
        out_shape=[
            jax.ShapeDtypeStruct((tiles // 2, states, states), jnp.bfloat16),
            jax.ShapeDtypeStruct((tiles // 2, states, states), jnp.float32),
        ],
        in_specs=[SMEM] * 2 + [VMEM] * len(received),
        out_specs=[VMEM] * 2,
        scratch_shapes=[pltpu.VMEM((tiles + 1, states, states), jnp.float32)],
        compiler_params=pltpu.CompilerParams(vmem_limit_bytes=16 * 1024 * 1024),
        name="gather",
    )(own_table, other_table, *received)


def cross_kernel(received, kept, give, keep):
    half = give.shape[0]
    x = lax.axis_index("mpo") // 2
    for j in range(half):
        away, here = (1 - x) * half + j, x * half + j
        give[j] = (kept[away] + received[away].astype(jnp.float32)).astype(jnp.bfloat16)
        keep[j] = kept[here] + received[here].astype(jnp.float32)


def cross(received, kept):
    half, states = kept.shape[0] // 2, kept.shape[1]
    return pl.pallas_call(
        cross_kernel,
        out_shape=[
            jax.ShapeDtypeStruct((half, states, states), jnp.bfloat16),
            jax.ShapeDtypeStruct((half, states, states), jnp.float32),
        ],
        in_specs=[VMEM] * 2,
        out_specs=[VMEM] * 2,
        compiler_params=pltpu.CompilerParams(vmem_limit_bytes=8 * 1024 * 1024),
        name="cross",
    )(received, kept)


def finish_kernel(tile_left, tile_right, left_sizes, right_sizes, received, kept, out):
    share, states = out.shape[0], out.shape[1]
    m = lax.axis_index("mpo")
    for j in range(share):
        h = m * share + j
        live = inside(states, left_sizes[tile_left[h]], right_sizes[tile_right[h]])
        out[j] = jnp.where(live, kept[j] + received[j].astype(jnp.float32), 0.0).astype(
            jnp.bfloat16
        )


def finish(tile_left, tile_right, left_sizes, right_sizes, received, kept):
    return pl.pallas_call(
        finish_kernel,
        out_shape=jax.ShapeDtypeStruct(kept.shape, jnp.bfloat16),
        in_specs=[SMEM] * 4 + [VMEM] * 2,
        out_specs=VMEM,
        compiler_params=pltpu.CompilerParams(vmem_limit_bytes=8 * 1024 * 1024),
        name="finish",
    )(tile_left, tile_right, left_sizes, right_sizes, received, kept)


def by_permutes(sizes, wave, left, right, left_sizes, right_sizes, tile_left, tile_right, send_slot, recv_tile):
    n_left, n_right, n_mpo = sizes
    axes = ("lsec", "rsec", "mpo")
    place = lambda z, y, m: (z * n_right + y) * n_mpo + m
    every = [(z, y, m) for z in range(n_left) for y in range(n_right) for m in range(n_mpo)]
    swap_core = [(m, m ^ 1) for m in range(n_mpo)]
    swap_chip = [(m, m ^ 2) for m in range(n_mpo)]
    other_table = lax.ppermute(recv_tile, "mpo", swap_core)

    def towards(flip):
        def order():
            z, y = lax.axis_index("lsec"), lax.axis_index("rsec")
            c = jnp.bitwise_xor(lax.rem(lax.axis_index("mpo"), 2), flip)
            return [
                jnp.bitwise_xor(z, k) * n_right + jnp.bitwise_xor(y, c) for k in range(n_left)
            ]

        return order

    give, keep = couple(
        [(towards(1), n_left), (towards(0), n_left)],
        n_left * n_right,
        tile_left, tile_right, left_sizes, right_sizes, send_slot, wave, left, right,
    )
    got = lax.ppermute(give, "mpo", swap_core)
    received = []
    for k in range(n_left):
        pair = jnp.stack([keep[k], got[k]])
        perm = [(place(z, y, m), place(z ^ k, y ^ (m % 2), m)) for z, y, m in every]
        received.append(lax.ppermute(pair, axes, perm))
    give, keep = gather(recv_tile, other_table, received, wave.shape[0])
    give, keep = cross(lax.ppermute(give, "mpo", swap_core), keep)
    return finish(
        tile_left, tile_right, left_sizes, right_sizes, lax.ppermute(give, "mpo", swap_chip), keep
    )


def by_exchange(sizes, wave, left, right, left_sizes, right_sizes, tile_left, tile_right, send_slot, recv_tile):
    peers = sizes[0] * sizes[1]
    tiles, states = wave.shape[0], wave.shape[1]
    (outgoing,) = couple(
        [(lambda: list(range(peers)), peers)],
        peers,
        tile_left, tile_right, left_sizes, right_sizes, send_slot, wave, left, right,
    )
    received = lax.all_to_all(outgoing, ("lsec", "rsec"), split_axis=0, concat_axis=0, tiled=True)
    chooser = (recv_tile[0][None, :] == jnp.arange(tiles, dtype=jnp.int32)[:, None]).astype(
        jnp.bfloat16
    )
    partial = jnp.dot(
        chooser, received.reshape(peers, states * states), preferred_element_type=jnp.float32
    )
    partial = partial.reshape(tiles, states, states).astype(jnp.bfloat16)
    share = lax.psum_scatter(partial, "mpo", scatter_dimension=0, tiled=True)
    start = lax.axis_index("mpo") * share.shape[0]
    at = lambda table, sizes_of: lax.dynamic_slice_in_dim(sizes_of[table], start, share.shape[0], 0)
    rows, cols = at(tile_left, left_sizes), at(tile_right, right_sizes)
    position = jnp.arange(states, dtype=jnp.int32)
    live = (position[None, :, None] < rows[:, None, None]) & (
        position[None, None, :] < cols[:, None, None]
    )
    return jnp.where(live, share, jnp.zeros_like(share))


def solution(mesh):
    sizes = tuple(mesh.shape[axis] for axis in ("lsec", "rsec", "mpo"))
    few = sizes[1] == 2 and sizes[2] == 4 and sizes[0] in (2, 4)
    placed = (
        P(("lsec", "rsec"), None, None),
        P("mpo", "lsec", None, None),
        P("mpo", "rsec", None, None),
        P("lsec"),
        P("rsec"),
        P(("lsec", "rsec")),
        P(("lsec", "rsec")),
        P("mpo", ("lsec", "rsec")),
        P("mpo", ("lsec", "rsec")),
    )
    return jax.shard_map(
        functools.partial(by_permutes if few else by_exchange, sizes),
        mesh=mesh,
        in_specs=placed,
        out_specs=P(("lsec", "rsec", "mpo"), None, None),
        check_vma=False,
    )
```

```python
import functools

import jax
import jax.numpy as jnp
from jax import lax
from jax.experimental import pallas as pl
from jax.experimental.pallas import tpu as pltpu
from jax.sharding import PartitionSpec as P

SMEM = pl.BlockSpec(memory_space=pltpu.SMEM)
VMEM = pl.BlockSpec(memory_space=pltpu.VMEM)
HBM = pl.BlockSpec(memory_space=pltpu.HBM)


def in_hbm(*arrays):
    return [pltpu.with_memory_space_constraint(x, pltpu.HBM) for x in arrays]


def inside(states, rows, cols):
    at_row = lax.broadcasted_iota(jnp.int32, (states, states), 0)
    at_col = lax.broadcasted_iota(jnp.int32, (states, states), 1)
    return (at_row < rows) & (at_col < cols)


def couple_kernel(groups, share, *refs):
    tables_hbm, (wave_hbm, left_hbm, right_hbm), rest = refs[:5], refs[5:8], refs[8:]
    outs, live, rest = rest[: len(groups)], rest[len(groups)], rest[len(groups) + 1 :]
    tables, rest = rest[:5], rest[5:]
    wave, left, right, masked, done, total, table_sem, wave_sem, left_sem, right_sem = rest
    tile_left, tile_right, left_sizes, right_sizes, send_slot = tables
    bonds, tiles, states = left.shape[0], wave.shape[0], wave.shape[1]
    step = done.shape[0] // tiles
    table_copies = [
        pltpu.make_async_copy(src, dst, table_sem.at[i])
        for i, (src, dst) in enumerate(zip(tables_hbm, tables))
    ]
    for copy in table_copies:
        copy.start()
    wave_copy = pltpu.make_async_copy(wave_hbm, wave, wave_sem)
    wave_copy.start()

    def copies(a):
        return (
            pltpu.make_async_copy(right_hbm.at[a], right.at[a], right_sem.at[a]),
            pltpu.make_async_copy(left_hbm.at[a], left.at[a], left_sem.at[a]),
        )

    for a in range(bonds):
        for copy in copies(a):
            copy.start()
    total[...] = jnp.zeros_like(total)
    for copy in table_copies:
        copy.wait()
    for j in range(live.shape[0]):
        h = share() + j
        keep = inside(states, left_sizes[tile_left[h]], right_sizes[tile_right[h]])
        live[j] = jnp.where(keep, 1.0, 0.0).astype(jnp.bfloat16)
    wave_copy.wait()
    for g in range(tiles):
        keep = inside(states, left_sizes[tile_left[g]], right_sizes[tile_right[g]])
        tile = wave[g].astype(jnp.float32)
        masked[g] = jnp.where(keep, tile, 0.0).astype(jnp.bfloat16)

    @pl.loop(0, bonds // step)
    def _(b):
        for u in range(step):
            for copy in copies(b * step + u):
                copy.wait()
        for g in range(tiles):
            blocks = jnp.concatenate([right[b * step + u, tile_right[g]] for u in range(step)], 0)
            wide = lax.dot_general(
                masked[g],
                blocks,
                (((1,), (1,)), ((), ())),
                preferred_element_type=jnp.float32,
            ).astype(jnp.bfloat16)
            for u in range(step):
                done[u * tiles + g] = wide[:, u * states : (u + 1) * states]
        for g in range(tiles):
            for u in range(step):
                total[send_slot[g, b * step + u]] += jnp.dot(
                    left[b * step + u, tile_left[g]],
                    done[u * tiles + g],
                    preferred_element_type=jnp.float32,
                )

    for out, order in zip(outs, groups):
        for j, q in enumerate(order()):
            out[j] = total[q].astype(jnp.bfloat16)


def couple(groups, share, peers, tile_left, tile_right, left_sizes, right_sizes, send_slot, wave, left, right):
    tiles, states = wave.shape[0], wave.shape[1]
    bonds = left.shape[0]
    step = max(d for d in range(1, 6) if bonds % d == 0)
    counts = [count for _, count in groups] + [share[1]]
    tables = (tile_left, tile_right, left_sizes, right_sizes, send_slot.T)
    return pl.pallas_call(
        functools.partial(couple_kernel, [g for g, _ in groups], share[0]),
        out_shape=[jax.ShapeDtypeStruct((count, states, states), jnp.bfloat16) for count in counts],
        in_specs=[HBM] * 8,
        out_specs=[VMEM] * len(counts),
        scratch_shapes=[pltpu.SMEM(table.shape, jnp.int32) for table in tables]
        + [
            pltpu.VMEM(wave.shape, jnp.bfloat16),
            pltpu.VMEM(left.shape, jnp.bfloat16),
            pltpu.VMEM(right.shape, jnp.bfloat16),
            pltpu.VMEM(wave.shape, jnp.bfloat16),
            pltpu.VMEM((step * tiles, states, states), jnp.bfloat16),
            pltpu.VMEM((peers + 1, states, states), jnp.float32),
            pltpu.SemaphoreType.DMA((len(tables),)),
            pltpu.SemaphoreType.DMA,
            pltpu.SemaphoreType.DMA((bonds,)),
            pltpu.SemaphoreType.DMA((bonds,)),
        ],
        compiler_params=pltpu.CompilerParams(vmem_limit_bytes=40 * 1024 * 1024),
        name="couple",
    )(*in_hbm(*tables, wave, left, right))


def gather_kernel(n_left, own_table, other_table, *rest):
    received = rest[:n_left]
    give, keep, total = rest[n_left:]
    z, y = lax.axis_index("lsec"), lax.axis_index("rsec")
    c = lax.rem(lax.axis_index("mpo"), 2)
    total[...] = jnp.zeros_like(total)
    for k in range(n_left):
        source = 2 * jnp.bitwise_xor(z, k) + jnp.bitwise_xor(y, c)
        for j, table in enumerate((own_table, other_table)):
            t = table[0, source]
            total[t] += received[k][j].astype(jnp.float32)
    quarter = (total.shape[0] - 1) // 4
    for x in range(2):
        for j in range(quarter):
            give[x * quarter + j] = total[(2 * x + 1 - c) * quarter + j].astype(jnp.bfloat16)
            keep[x * quarter + j] = total[(2 * x + c) * quarter + j]


def gather(own_table, other_table, received, tiles):
    states = received[0].shape[1]
    return pl.pallas_call(
        functools.partial(gather_kernel, len(received)),
        out_shape=[
            jax.ShapeDtypeStruct((tiles // 2, states, states), jnp.bfloat16),
            jax.ShapeDtypeStruct((tiles // 2, states, states), jnp.float32),
        ],
        in_specs=[SMEM] * 2 + [VMEM] * len(received),
        out_specs=[VMEM] * 2,
        scratch_shapes=[pltpu.VMEM((tiles + 1, states, states), jnp.float32)],
        compiler_params=pltpu.CompilerParams(vmem_limit_bytes=16 * 1024 * 1024),
        name="gather",
    )(own_table, other_table, *received)


def cross_kernel(received, kept, give, keep):
    half = give.shape[0]
    x = lax.axis_index("mpo") // 2
    for j in range(half):
        away, here = (1 - x) * half + j, x * half + j
        give[j] = (kept[away] + received[away].astype(jnp.float32)).astype(jnp.bfloat16)
        keep[j] = kept[here] + received[here].astype(jnp.float32)


def cross(received, kept):
    half, states = kept.shape[0] // 2, kept.shape[1]
    return pl.pallas_call(
        cross_kernel,
        out_shape=[
            jax.ShapeDtypeStruct((half, states, states), jnp.bfloat16),
            jax.ShapeDtypeStruct((half, states, states), jnp.float32),
        ],
        in_specs=[VMEM] * 2,
        out_specs=[VMEM] * 2,
        compiler_params=pltpu.CompilerParams(vmem_limit_bytes=8 * 1024 * 1024),
        name="cross",
    )(received, kept)


def by_permutes(sizes, wave, left, right, left_sizes, right_sizes, tile_left, tile_right, send_slot, recv_tile):
    n_left, n_right, n_mpo = sizes
    axes = ("lsec", "rsec", "mpo")
    place = lambda z, y, m: (z * n_right + y) * n_mpo + m
    every = [(z, y, m) for z in range(n_left) for y in range(n_right) for m in range(n_mpo)]
    swap_core = [(m, m ^ 1) for m in range(n_mpo)]
    swap_chip = [(m, m ^ 2) for m in range(n_mpo)]
    other_table = lax.ppermute(recv_tile, "mpo", swap_core)

    def towards(flip):
        def order():
            z, y = lax.axis_index("lsec"), lax.axis_index("rsec")
            c = jnp.bitwise_xor(lax.rem(lax.axis_index("mpo"), 2), flip)
            return [
                jnp.bitwise_xor(z, k) * n_right + jnp.bitwise_xor(y, c) for k in range(n_left)
            ]

        return order

    share = wave.shape[0] // n_mpo
    give, keep, live = couple(
        [(towards(1), n_left), (towards(0), n_left)],
        (lambda: lax.axis_index("mpo") * share, share),
        n_left * n_right,
        tile_left, tile_right, left_sizes, right_sizes, send_slot, wave, left, right,
    )
    give, other_table = lax.optimization_barrier((give, other_table))
    got = lax.ppermute(give, "mpo", swap_core)
    received = []
    for k in range(n_left):
        pair = jnp.stack([keep[k], got[k]])
        perm = [(place(z, y, m), place(z ^ k, y ^ (m % 2), m)) for z, y, m in every]
        received.append(lax.ppermute(pair, axes, perm))
    give, keep = gather(recv_tile, other_table, received, wave.shape[0])
    give, keep = cross(lax.ppermute(give, "mpo", swap_core), keep)
    summed = keep + lax.ppermute(give, "mpo", swap_chip).astype(jnp.float32)
    return jnp.where(live > 0, summed, 0.0).astype(jnp.bfloat16)


def by_exchange(sizes, wave, left, right, left_sizes, right_sizes, tile_left, tile_right, send_slot, recv_tile):
    peers = sizes[0] * sizes[1]
    tiles, states = wave.shape[0], wave.shape[1]
    share = tiles // sizes[2]
    outgoing, live = couple(
        [(lambda: list(range(peers)), peers)],
        (lambda: lax.axis_index("mpo") * share, share),
        peers,
        tile_left, tile_right, left_sizes, right_sizes, send_slot, wave, left, right,
    )
    received = lax.all_to_all(outgoing, ("lsec", "rsec"), split_axis=0, concat_axis=0, tiled=True)
    chooser = (recv_tile[0][None, :] == jnp.arange(tiles, dtype=jnp.int32)[:, None]).astype(
        jnp.bfloat16
    )
    partial = jnp.dot(
        chooser, received.reshape(peers, states * states), preferred_element_type=jnp.float32
    )
    partial = partial.reshape(tiles, states, states).astype(jnp.bfloat16)
    mine = lax.psum_scatter(partial, "mpo", scatter_dimension=0, tiled=True)
    return jnp.where(live > 0, mine, jnp.zeros_like(mine))


def solution(mesh):
    sizes = tuple(mesh.shape[axis] for axis in ("lsec", "rsec", "mpo"))
    few = sizes[1] == 2 and sizes[2] == 4 and sizes[0] in (2, 4)
    placed = (
        P(("lsec", "rsec"), None, None),
        P("mpo", "lsec", None, None),
        P("mpo", "rsec", None, None),
        P("lsec"),
        P("rsec"),
        P(("lsec", "rsec")),
        P(("lsec", "rsec")),
        P("mpo", ("lsec", "rsec")),
        P("mpo", ("lsec", "rsec")),
    )
    return jax.shard_map(
        functools.partial(by_permutes if few else by_exchange, sizes),
        mesh=mesh,
        in_specs=placed,
        out_specs=P(("lsec", "rsec", "mpo"), None, None),
        check_vma=False,
    )
```

```python
import functools

import jax
import jax.numpy as jnp
from jax import lax
from jax.experimental import pallas as pl
from jax.experimental.pallas import tpu as pltpu
from jax.sharding import PartitionSpec as P

SMEM = pl.BlockSpec(memory_space=pltpu.SMEM)
VMEM = pl.BlockSpec(memory_space=pltpu.VMEM)
HBM = pl.BlockSpec(memory_space=pltpu.HBM)


def in_hbm(*arrays):
    return [pltpu.with_memory_space_constraint(x, pltpu.HBM) for x in arrays]


def inside(states, rows, cols):
    at_row = lax.broadcasted_iota(jnp.int32, (states, states), 0)
    at_col = lax.broadcasted_iota(jnp.int32, (states, states), 1)
    return (at_row < rows) & (at_col < cols)


def couple_kernel(groups, share, *refs):
    tables_hbm, (wave_hbm, left_hbm, right_hbm), rest = refs[:5], refs[5:8], refs[8:]
    outs, live, rest = rest[: len(groups)], rest[len(groups)], rest[len(groups) + 1 :]
    tables, rest = rest[:5], rest[5:]
    wave, left, right, masked, done, total, table_sem, wave_sem, left_sem, right_sem = rest
    tile_left, tile_right, left_sizes, right_sizes, send_slot = tables
    bonds, tiles, states = left.shape[0], wave.shape[0], wave.shape[1]
    table_copies = [
        pltpu.make_async_copy(src, dst, table_sem.at[i])
        for i, (src, dst) in enumerate(zip(tables_hbm, tables))
    ]
    for copy in table_copies:
        copy.start()
    wave_copy = pltpu.make_async_copy(wave_hbm, wave, wave_sem)
    wave_copy.start()
    right_copy = pltpu.make_async_copy(right_hbm, right, right_sem)
    right_copy.start()
    total[...] = jnp.zeros_like(total)
    for copy in table_copies:
        copy.wait()
    left_copy = pltpu.make_async_copy(left_hbm, left, left_sem)
    left_copy.start()
    for j in range(live.shape[0]):
        h = share() + j
        keep = inside(states, left_sizes[tile_left[h]], right_sizes[tile_right[h]])
        live[j] = jnp.where(keep, 1.0, 0.0).astype(jnp.bfloat16)
    wave_copy.wait()
    for g in range(tiles):
        keep = inside(states, left_sizes[tile_left[g]], right_sizes[tile_right[g]])
        tile = wave[g].astype(jnp.float32)
        masked[g] = jnp.where(keep, tile, 0.0).astype(jnp.bfloat16)
    right_copy.wait()
    for g in range(tiles):
        blocks = jnp.concatenate([right[a, tile_right[g]] for a in range(bonds)], 0)
        wide = lax.dot_general(
            masked[g], blocks, (((1,), (1,)), ((), ())), preferred_element_type=jnp.float32
        ).astype(jnp.bfloat16)
        for a in range(bonds):
            done[a * tiles + g] = wide[:, a * states : (a + 1) * states]
    left_copy.wait()
    for g in range(tiles):
        for a in range(bonds):
            total[send_slot[g, a]] += jnp.dot(
                left[a, tile_left[g]], done[a * tiles + g], preferred_element_type=jnp.float32
            )

    for out, order in zip(outs, groups):
        for j, q in enumerate(order()):
            out[j] = total[q].astype(jnp.bfloat16)


def couple(groups, share, peers, tile_left, tile_right, left_sizes, right_sizes, send_slot, wave, left, right):
    tiles, states = wave.shape[0], wave.shape[1]
    bonds = left.shape[0]
    counts = [count for _, count in groups] + [share[1]]
    tables = (tile_left, tile_right, left_sizes, right_sizes, send_slot.T)
    return pl.pallas_call(
        functools.partial(couple_kernel, [g for g, _ in groups], share[0]),
        out_shape=[jax.ShapeDtypeStruct((count, states, states), jnp.bfloat16) for count in counts],
        in_specs=[HBM] * 8,
        out_specs=[VMEM] * len(counts),
        scratch_shapes=[pltpu.SMEM(table.shape, jnp.int32) for table in tables]
        + [
            pltpu.VMEM(wave.shape, jnp.bfloat16),
            pltpu.VMEM(left.shape, jnp.bfloat16),
            pltpu.VMEM(right.shape, jnp.bfloat16),
            pltpu.VMEM(wave.shape, jnp.bfloat16),
            pltpu.VMEM((bonds * tiles, states, states), jnp.bfloat16),
            pltpu.VMEM((peers + 1, states, states), jnp.float32),
            pltpu.SemaphoreType.DMA((len(tables),)),
            pltpu.SemaphoreType.DMA,
            pltpu.SemaphoreType.DMA,
            pltpu.SemaphoreType.DMA,
        ],
        compiler_params=pltpu.CompilerParams(vmem_limit_bytes=40 * 1024 * 1024),
        name="couple",
    )(*in_hbm(*tables, wave, left, right))


SETS = (((3, 0), (2, 0), (1, 0)), ((2, 1), (1, 1), (0, 1)))
FAR = (3, 1)


def flipped(core, i):
    z, y = lax.axis_index("lsec"), lax.axis_index("rsec")
    dz, dy = (jnp.where(core == 0, SETS[0][i][d], SETS[1][i][d]) for d in range(2))
    return jnp.bitwise_xor(z, dz) * 2 + jnp.bitwise_xor(y, dy)


def fixed(dz, dy):
    z, y = lax.axis_index("lsec"), lax.axis_index("rsec")
    return jnp.bitwise_xor(z, dz) * 2 + jnp.bitwise_xor(y, dy)


def first_kernel(own_table, other_table, received, held, part, chosen, total):
    core = lax.rem(lax.axis_index("mpo"), 2)
    quarter = (total.shape[0] - 1) // 4
    total[...] = jnp.zeros_like(total)
    total[own_table[0, fixed(0, 0)]] = held[0].astype(jnp.float32)
    source = flipped(core, 0)
    total[own_table[0, source]] += received[0].astype(jnp.float32)
    total[other_table[0, source]] += received[1].astype(jnp.float32)
    targets = [table[0, flipped(core, i)] for i in (1, 2) for table in (own_table, other_table)]
    targets.append(own_table[0, fixed(*FAR)])
    for side, half in enumerate((1 - core, core)):
        for x in range(2):
            for j in range(quarter):
                at = (side * 2 + x) * quarter + j
                tile = (2 * x + half) * quarter + j
                part[at] = total[tile]
                for s, target in enumerate(targets):
                    one = jnp.where(target == tile, 1.0, 0.0)
                    chosen[s, at] = jnp.full(chosen.shape[2:], one, jnp.float32)


def second_kernel(part, chosen, near, nearest, far, give, keep):
    slots = [near[0], near[1], nearest[0], nearest[1], far[0]]
    half, states = give.shape[0], give.shape[1]
    for at in range(2 * half):
        tile = part[at].reshape(states // 8, 8, states)
        for s, slot in enumerate(slots):
            rows = slot.astype(jnp.float32).reshape(states // 8, 8, states)
            tile += rows * chosen[s, at][None]
        tile = tile.reshape(states, states)
        if at < half:
            give[at] = tile.astype(jnp.bfloat16)
        else:
            keep[at - half] = tile


def gather(own_table, other_table, held, longest, near, nearest, far, tiles):
    states = held.shape[1]
    whole = (tiles, states, states)
    part, chosen = pl.pallas_call(
        first_kernel,
        out_shape=[
            jax.ShapeDtypeStruct(whole, jnp.float32),
            jax.ShapeDtypeStruct((5, tiles, 8, states), jnp.float32),
        ],
        in_specs=[SMEM] * 2 + [VMEM] * 2,
        out_specs=[VMEM] * 2,
        scratch_shapes=[pltpu.VMEM((tiles + 1, states, states), jnp.float32)],
        compiler_params=pltpu.CompilerParams(vmem_limit_bytes=16 * 1024 * 1024),
        name="first_sums",
    )(own_table, other_table, longest, held)
    return pl.pallas_call(
        second_kernel,
        out_shape=[
            jax.ShapeDtypeStruct((tiles // 2, states, states), jnp.bfloat16),
            jax.ShapeDtypeStruct((tiles // 2, states, states), jnp.float32),
        ],
        in_specs=[VMEM] * 5,
        out_specs=[VMEM] * 2,
        compiler_params=pltpu.CompilerParams(vmem_limit_bytes=16 * 1024 * 1024),
        name="second_sums",
    )(part, chosen, near, nearest, far)


def cross_kernel(received, kept, give, keep):
    half = give.shape[0]
    x = lax.axis_index("mpo") // 2
    for j in range(half):
        away, here = (1 - x) * half + j, x * half + j
        give[j] = (kept[away] + received[away].astype(jnp.float32)).astype(jnp.bfloat16)
        keep[j] = kept[here] + received[here].astype(jnp.float32)


def cross(received, kept):
    half, states = kept.shape[0] // 2, kept.shape[1]
    return pl.pallas_call(
        cross_kernel,
        out_shape=[
            jax.ShapeDtypeStruct((half, states, states), jnp.bfloat16),
            jax.ShapeDtypeStruct((half, states, states), jnp.float32),
        ],
        in_specs=[VMEM] * 2,
        out_specs=[VMEM] * 2,
        compiler_params=pltpu.CompilerParams(vmem_limit_bytes=8 * 1024 * 1024),
        name="cross",
    )(received, kept)


def by_permutes(sizes, wave, left, right, left_sizes, right_sizes, tile_left, tile_right, send_slot, recv_tile):
    n_left, n_right, n_mpo = sizes
    axes = ("lsec", "rsec", "mpo")
    place = lambda z, y, m: (z * n_right + y) * n_mpo + m
    every = [(z, y, m) for z in range(n_left) for y in range(n_right) for m in range(n_mpo)]
    swap_core = [(m, m ^ 1) for m in range(n_mpo)]
    swap_chip = [(m, m ^ 2) for m in range(n_mpo)]
    other_table = lax.ppermute(recv_tile, "mpo", swap_core)

    share = wave.shape[0] // n_mpo
    core = lambda flip: jnp.bitwise_xor(lax.rem(lax.axis_index("mpo"), 2), flip)
    give, keep, far, held, live = couple(
        [
            (lambda: [flipped(core(1), i) for i in range(3)], 3),
            (lambda: [flipped(core(0), i) for i in range(3)], 3),
            (lambda: [fixed(*FAR)], 1),
            (lambda: [fixed(0, 0)], 1),
        ],
        (lambda: lax.axis_index("mpo") * share, share),
        n_left * n_right,
        tile_left, tile_right, left_sizes, right_sizes, send_slot, wave, left, right,
    )

    def move(x, flips):
        perm = [
            (place(z, y, m), place(z ^ flips[m % 2][0], y ^ flips[m % 2][1], m))
            for z, y, m in every
        ]
        return lax.ppermute(x, axes, perm)

    give, other_table = lax.optimization_barrier((give, other_table))
    got = lax.ppermute(give, "mpo", swap_core)
    far = move(far, (FAR, FAR))
    received = [
        move(jnp.stack([keep[i], got[i]]), (SETS[0][i], SETS[1][i])) for i in range(3)
    ]
    give, keep = gather(recv_tile, other_table, held, *received, far, wave.shape[0])
    give, keep = cross(lax.ppermute(give, "mpo", swap_core), keep)
    summed = keep + lax.ppermute(give, "mpo", swap_chip).astype(jnp.float32)
    return jnp.where(live > 0, summed, 0.0).astype(jnp.bfloat16)


def by_exchange(sizes, wave, left, right, left_sizes, right_sizes, tile_left, tile_right, send_slot, recv_tile):
    peers = sizes[0] * sizes[1]
    tiles, states = wave.shape[0], wave.shape[1]
    share = tiles // sizes[2]
    outgoing, live = couple(
        [(lambda: list(range(peers)), peers)],
        (lambda: lax.axis_index("mpo") * share, share),
        peers,
        tile_left, tile_right, left_sizes, right_sizes, send_slot, wave, left, right,
    )
    received = lax.all_to_all(outgoing, ("lsec", "rsec"), split_axis=0, concat_axis=0, tiled=True)
    chooser = (recv_tile[0][None, :] == jnp.arange(tiles, dtype=jnp.int32)[:, None]).astype(
        jnp.bfloat16
    )
    partial = jnp.dot(
        chooser, received.reshape(peers, states * states), preferred_element_type=jnp.float32
    )
    partial = partial.reshape(tiles, states, states).astype(jnp.bfloat16)
    mine = lax.psum_scatter(partial, "mpo", scatter_dimension=0, tiled=True)
    return jnp.where(live > 0, mine, jnp.zeros_like(mine))


def solution(mesh):
    sizes = tuple(mesh.shape[axis] for axis in ("lsec", "rsec", "mpo"))
    few = sizes == (4, 2, 4)
    placed = (
        P(("lsec", "rsec"), None, None),
        P("mpo", "lsec", None, None),
        P("mpo", "rsec", None, None),
        P("lsec"),
        P("rsec"),
        P(("lsec", "rsec")),
        P(("lsec", "rsec")),
        P("mpo", ("lsec", "rsec")),
        P("mpo", ("lsec", "rsec")),
    )
    return jax.shard_map(
        functools.partial(by_permutes if few else by_exchange, sizes),
        mesh=mesh,
        in_specs=placed,
        out_specs=P(("lsec", "rsec", "mpo"), None, None),
        check_vma=False,
    )
```

```python
import functools

import jax
import jax.numpy as jnp
from jax import lax
from jax.experimental import pallas as pl
from jax.experimental.pallas import tpu as pltpu
from jax.sharding import PartitionSpec as P

SMEM = pl.BlockSpec(memory_space=pltpu.SMEM)
VMEM = pl.BlockSpec(memory_space=pltpu.VMEM)
HBM = pl.BlockSpec(memory_space=pltpu.HBM)


def in_hbm(*arrays):
    return [pltpu.with_memory_space_constraint(x, pltpu.HBM) for x in arrays]


def inside(states, rows, cols):
    at_row = lax.broadcasted_iota(jnp.int32, (states, states), 0)
    at_col = lax.broadcasted_iota(jnp.int32, (states, states), 1)
    return (at_row < rows) & (at_col < cols)


def couple_kernel(groups, share, *refs):
    tables_hbm, (wave_hbm, left_hbm, right_hbm), rest = refs[:5], refs[5:8], refs[8:]
    outs, live, rest = rest[: len(groups)], rest[len(groups)], rest[len(groups) + 1 :]
    tables, rest = rest[:5], rest[5:]
    wave, left, right, masked, done, total, table_sem, wave_sem, left_sem, right_sem = rest
    tile_left, tile_right, left_sizes, right_sizes, send_slot = tables
    bonds, tiles, states = left.shape[0], wave.shape[0], wave.shape[1]
    table_copies = [
        pltpu.make_async_copy(src, dst, table_sem.at[i])
        for i, (src, dst) in enumerate(zip(tables_hbm, tables))
    ]
    for copy in table_copies:
        copy.start()
    wave_copy = pltpu.make_async_copy(wave_hbm, wave, wave_sem)
    wave_copy.start()
    right_copy = pltpu.make_async_copy(right_hbm, right, right_sem)
    right_copy.start()
    total[...] = jnp.zeros_like(total)
    for copy in table_copies:
        copy.wait()
    left_copy = pltpu.make_async_copy(left_hbm, left, left_sem)
    left_copy.start()
    for j in range(live.shape[0]):
        h = share() + j
        keep = inside(states, left_sizes[tile_left[h]], right_sizes[tile_right[h]])
        live[j] = jnp.where(keep, 1.0, 0.0).astype(jnp.bfloat16)
    wave_copy.wait()
    for g in range(tiles):
        keep = inside(states, left_sizes[tile_left[g]], right_sizes[tile_right[g]])
        tile = wave[g].astype(jnp.float32)
        masked[g] = jnp.where(keep, tile, 0.0).astype(jnp.bfloat16)
    right_copy.wait()
    for g in range(tiles):
        blocks = jnp.concatenate([right[a, tile_right[g]] for a in range(bonds)], 0)
        wide = lax.dot_general(
            masked[g], blocks, (((1,), (1,)), ((), ())), preferred_element_type=jnp.float32
        ).astype(jnp.bfloat16)
        for a in range(bonds):
            done[a * tiles + g] = wide[:, a * states : (a + 1) * states]
    left_copy.wait()
    for g in range(tiles):
        for a in range(bonds):
            total[send_slot[g, a]] += jnp.dot(
                left[a, tile_left[g]], done[a * tiles + g], preferred_element_type=jnp.float32
            )

    for out, order in zip(outs, groups):
        for j, q in enumerate(order()):
            out[j] = total[q].astype(jnp.bfloat16)


def couple(groups, share, peers, tile_left, tile_right, left_sizes, right_sizes, send_slot, wave, left, right):
    tiles, states = wave.shape[0], wave.shape[1]
    bonds = left.shape[0]
    counts = [count for _, count in groups] + [share[1]]
    tables = (tile_left, tile_right, left_sizes, right_sizes, send_slot.T)
    return pl.pallas_call(
        functools.partial(couple_kernel, [g for g, _ in groups], share[0]),
        out_shape=[jax.ShapeDtypeStruct((count, states, states), jnp.bfloat16) for count in counts],
        in_specs=[HBM] * 8,
        out_specs=[VMEM] * len(counts),
        scratch_shapes=[pltpu.SMEM(table.shape, jnp.int32) for table in tables]
        + [
            pltpu.VMEM(wave.shape, jnp.bfloat16),
            pltpu.VMEM(left.shape, jnp.bfloat16),
            pltpu.VMEM(right.shape, jnp.bfloat16),
            pltpu.VMEM(wave.shape, jnp.bfloat16),
            pltpu.VMEM((bonds * tiles, states, states), jnp.bfloat16),
            pltpu.VMEM((peers + 1, states, states), jnp.float32),
            pltpu.SemaphoreType.DMA((len(tables),)),
            pltpu.SemaphoreType.DMA,
            pltpu.SemaphoreType.DMA,
            pltpu.SemaphoreType.DMA,
        ],
        compiler_params=pltpu.CompilerParams(vmem_limit_bytes=40 * 1024 * 1024),
        name="couple",
    )(*in_hbm(*tables, wave, left, right))


SETS = (((3, 0), (2, 0), (1, 0)), ((2, 1), (1, 1), (0, 1)))
FAR = (3, 1)


def flipped(core, i):
    z, y = lax.axis_index("lsec"), lax.axis_index("rsec")
    dz, dy = (jnp.where(core == 0, SETS[0][i][d], SETS[1][i][d]) for d in range(2))
    return jnp.bitwise_xor(z, dz) * 2 + jnp.bitwise_xor(y, dy)


def fixed(dz, dy):
    z, y = lax.axis_index("lsec"), lax.axis_index("rsec")
    return jnp.bitwise_xor(z, dz) * 2 + jnp.bitwise_xor(y, dy)


def first_kernel(own_table, other_table, received, held, part, chosen, total):
    core = lax.rem(lax.axis_index("mpo"), 2)
    quarter = (total.shape[0] - 1) // 4
    total[...] = jnp.zeros_like(total)
    total[own_table[0, fixed(0, 0)]] = held[0].astype(jnp.float32)
    total[own_table[0, fixed(*FAR)]] += received[0].astype(jnp.float32)
    targets = [table[0, flipped(core, i)] for i in range(3) for table in (own_table, other_table)]
    for side, half in enumerate((1 - core, core)):
        for x in range(2):
            for j in range(quarter):
                at = (side * 2 + x) * quarter + j
                tile = (2 * x + half) * quarter + j
                part[at] = total[tile]
                for s, target in enumerate(targets):
                    one = jnp.where(target == tile, 1.0, 0.0)
                    chosen[s, at] = jnp.full(chosen.shape[2:], one, jnp.float32)


def second_kernel(part, chosen, long, near, nearest, give, keep):
    slots = [long[0], long[1], near[0], near[1], nearest[0], nearest[1]]
    half, states = give.shape[0], give.shape[1]
    for at in range(2 * half):
        tile = part[at].reshape(states // 8, 8, states)
        for s, slot in enumerate(slots):
            rows = slot.astype(jnp.float32).reshape(states // 8, 8, states)
            tile += rows * chosen[s, at][None]
        tile = tile.reshape(states, states)
        if at < half:
            give[at] = tile.astype(jnp.bfloat16)
        else:
            keep[at - half] = tile


def gather(own_table, other_table, held, longest, near, nearest, far, tiles):
    states = held.shape[1]
    whole = (tiles, states, states)
    part, chosen = pl.pallas_call(
        first_kernel,
        out_shape=[
            jax.ShapeDtypeStruct(whole, jnp.float32),
            jax.ShapeDtypeStruct((6, tiles, 8, states), jnp.float32),
        ],
        in_specs=[SMEM] * 2 + [VMEM] * 2,
        out_specs=[VMEM] * 2,
        scratch_shapes=[pltpu.VMEM((tiles + 1, states, states), jnp.float32)],
        compiler_params=pltpu.CompilerParams(vmem_limit_bytes=16 * 1024 * 1024),
        name="first_sums",
        cost_estimate=pl.CostEstimate(flops=2 * 10**9, bytes_accessed=10**6, transcendentals=0),
    )(own_table, other_table, far, held)
    return pl.pallas_call(
        second_kernel,
        out_shape=[
            jax.ShapeDtypeStruct((tiles // 2, states, states), jnp.bfloat16),
            jax.ShapeDtypeStruct((tiles // 2, states, states), jnp.float32),
        ],
        in_specs=[VMEM] * 5,
        out_specs=[VMEM] * 2,
        compiler_params=pltpu.CompilerParams(vmem_limit_bytes=16 * 1024 * 1024),
        name="second_sums",
    )(part, chosen, longest, near, nearest)


def cross_kernel(received, kept, give, keep):
    half = give.shape[0]
    x = lax.axis_index("mpo") // 2
    for j in range(half):
        away, here = (1 - x) * half + j, x * half + j
        give[j] = (kept[away] + received[away].astype(jnp.float32)).astype(jnp.bfloat16)
        keep[j] = kept[here] + received[here].astype(jnp.float32)


def cross(received, kept):
    half, states = kept.shape[0] // 2, kept.shape[1]
    return pl.pallas_call(
        cross_kernel,
        out_shape=[
            jax.ShapeDtypeStruct((half, states, states), jnp.bfloat16),
            jax.ShapeDtypeStruct((half, states, states), jnp.float32),
        ],
        in_specs=[VMEM] * 2,
        out_specs=[VMEM] * 2,
        compiler_params=pltpu.CompilerParams(vmem_limit_bytes=8 * 1024 * 1024),
        name="cross",
    )(received, kept)


def by_permutes(sizes, wave, left, right, left_sizes, right_sizes, tile_left, tile_right, send_slot, recv_tile):
    n_left, n_right, n_mpo = sizes
    axes = ("lsec", "rsec", "mpo")
    place = lambda z, y, m: (z * n_right + y) * n_mpo + m
    every = [(z, y, m) for z in range(n_left) for y in range(n_right) for m in range(n_mpo)]
    swap_core = [(m, m ^ 1) for m in range(n_mpo)]
    swap_chip = [(m, m ^ 2) for m in range(n_mpo)]
    other_table = lax.ppermute(recv_tile, "mpo", swap_core)

    share = wave.shape[0] // n_mpo
    core = lambda flip: jnp.bitwise_xor(lax.rem(lax.axis_index("mpo"), 2), flip)
    give, rest, live = couple(
        [
            (lambda: [flipped(core(1), i) for i in range(3)], 3),
            (
                lambda: [flipped(core(0), i) for i in range(3)] + [fixed(*FAR), fixed(0, 0)],
                5,
            ),
        ],
        (lambda: lax.axis_index("mpo") * share, share),
        n_left * n_right,
        tile_left, tile_right, left_sizes, right_sizes, send_slot, wave, left, right,
    )

    def move(x, flips):
        perm = [
            (place(z, y, m), place(z ^ flips[m % 2][0], y ^ flips[m % 2][1], m))
            for z, y, m in every
        ]
        return lax.ppermute(x, axes, perm)

    give, other_table = lax.optimization_barrier((give, other_table))
    got = lax.ppermute(give, "mpo", swap_core)
    keep, far, held = rest[:3], rest[3:4], rest[4:]
    far = move(far, (FAR, FAR))
    received = [
        move(jnp.stack([keep[i], got[i]]), (SETS[0][i], SETS[1][i])) for i in range(3)
    ]
    give, keep = gather(recv_tile, other_table, held, *received, far, wave.shape[0])
    give, keep = cross(lax.ppermute(give, "mpo", swap_core), keep)
    summed = keep + lax.ppermute(give, "mpo", swap_chip).astype(jnp.float32)
    return jnp.where(live > 0, summed, 0.0).astype(jnp.bfloat16)


def by_exchange(sizes, wave, left, right, left_sizes, right_sizes, tile_left, tile_right, send_slot, recv_tile):
    peers = sizes[0] * sizes[1]
    tiles, states = wave.shape[0], wave.shape[1]
    share = tiles // sizes[2]
    outgoing, live = couple(
        [(lambda: list(range(peers)), peers)],
        (lambda: lax.axis_index("mpo") * share, share),
        peers,
        tile_left, tile_right, left_sizes, right_sizes, send_slot, wave, left, right,
    )
    received = lax.all_to_all(outgoing, ("lsec", "rsec"), split_axis=0, concat_axis=0, tiled=True)
    chooser = (recv_tile[0][None, :] == jnp.arange(tiles, dtype=jnp.int32)[:, None]).astype(
        jnp.bfloat16
    )
    partial = jnp.dot(
        chooser, received.reshape(peers, states * states), preferred_element_type=jnp.float32
    )
    partial = partial.reshape(tiles, states, states).astype(jnp.bfloat16)
    mine = lax.psum_scatter(partial, "mpo", scatter_dimension=0, tiled=True)
    return jnp.where(live > 0, mine, jnp.zeros_like(mine))


def solution(mesh):
    sizes = tuple(mesh.shape[axis] for axis in ("lsec", "rsec", "mpo"))
    few = sizes == (4, 2, 4)
    placed = (
        P(("lsec", "rsec"), None, None),
        P("mpo", "lsec", None, None),
        P("mpo", "rsec", None, None),
        P("lsec"),
        P("rsec"),
        P(("lsec", "rsec")),
        P(("lsec", "rsec")),
        P("mpo", ("lsec", "rsec")),
        P("mpo", ("lsec", "rsec")),
    )
    return jax.shard_map(
        functools.partial(by_permutes if few else by_exchange, sizes),
        mesh=mesh,
        in_specs=placed,
        out_specs=P(("lsec", "rsec", "mpo"), None, None),
        check_vma=False,
    )
```

```python
import functools

import jax
import jax.numpy as jnp
from jax import lax
from jax.experimental import pallas as pl
from jax.experimental.pallas import tpu as pltpu
from jax.sharding import PartitionSpec as P

SMEM = pl.BlockSpec(memory_space=pltpu.SMEM)
VMEM = pl.BlockSpec(memory_space=pltpu.VMEM)
HBM = pl.BlockSpec(memory_space=pltpu.HBM)


def in_hbm(*arrays):
    return [pltpu.with_memory_space_constraint(x, pltpu.HBM) for x in arrays]


def inside(states, rows, cols):
    at_row = lax.broadcasted_iota(jnp.int32, (states, states), 0)
    at_col = lax.broadcasted_iota(jnp.int32, (states, states), 1)
    return (at_row < rows) & (at_col < cols)


def couple_kernel(groups, share, *refs):
    tables_hbm, (wave_hbm, left_hbm, right_hbm), rest = refs[:5], refs[5:8], refs[8:]
    outs, live, rest = rest[: len(groups)], rest[len(groups)], rest[len(groups) + 1 :]
    tables, rest = rest[:5], rest[5:]
    wave, left, right, masked, done, total, table_sem, wave_sem, left_sem, right_sem = rest
    tile_left, tile_right, left_sizes, right_sizes, send_slot = tables
    bonds, tiles, states = left.shape[0], wave.shape[0], wave.shape[1]
    table_copies = [
        pltpu.make_async_copy(src, dst, table_sem.at[i])
        for i, (src, dst) in enumerate(zip(tables_hbm, tables))
    ]
    for copy in table_copies:
        copy.start()
    wave_copy = pltpu.make_async_copy(wave_hbm, wave, wave_sem)
    wave_copy.start()
    right_copy = pltpu.make_async_copy(right_hbm, right, right_sem)
    right_copy.start()
    total[...] = jnp.zeros_like(total)
    for copy in table_copies:
        copy.wait()
    left_copy = pltpu.make_async_copy(left_hbm, left, left_sem)
    left_copy.start()
    for j in range(live.shape[0]):
        h = share() + j
        keep = inside(states, left_sizes[tile_left[h]], right_sizes[tile_right[h]])
        live[j] = jnp.where(keep, 1.0, 0.0).astype(jnp.bfloat16)
    wave_copy.wait()
    for g in range(tiles):
        keep = inside(states, left_sizes[tile_left[g]], right_sizes[tile_right[g]])
        tile = wave[g].astype(jnp.float32)
        masked[g] = jnp.where(keep, tile, 0.0).astype(jnp.bfloat16)
    right_copy.wait()
    for g in range(tiles):
        blocks = jnp.concatenate([right[a, tile_right[g]] for a in range(bonds)], 0)
        wide = lax.dot_general(
            masked[g], blocks, (((1,), (1,)), ((), ())), preferred_element_type=jnp.float32
        ).astype(jnp.bfloat16)
        for a in range(bonds):
            done[a * tiles + g] = wide[:, a * states : (a + 1) * states]
    left_copy.wait()
    for g in range(tiles):
        for a in range(bonds):
            total[send_slot[g, a]] += jnp.dot(
                left[a, tile_left[g]], done[a * tiles + g], preferred_element_type=jnp.float32
            )

    for out, order in zip(outs, groups):
        for j, q in enumerate(order()):
            out[j] = total[q].astype(jnp.bfloat16)


def couple(groups, share, peers, tile_left, tile_right, left_sizes, right_sizes, send_slot, wave, left, right):
    tiles, states = wave.shape[0], wave.shape[1]
    bonds = left.shape[0]
    counts = [count for _, count in groups] + [share[1]]
    tables = (tile_left, tile_right, left_sizes, right_sizes, send_slot.T)
    return pl.pallas_call(
        functools.partial(couple_kernel, [g for g, _ in groups], share[0]),
        out_shape=[jax.ShapeDtypeStruct((count, states, states), jnp.bfloat16) for count in counts],
        in_specs=[HBM] * 8,
        out_specs=[VMEM] * len(counts),
        scratch_shapes=[pltpu.SMEM(table.shape, jnp.int32) for table in tables]
        + [
            pltpu.VMEM(wave.shape, jnp.bfloat16),
            pltpu.VMEM(left.shape, jnp.bfloat16),
            pltpu.VMEM(right.shape, jnp.bfloat16),
            pltpu.VMEM(wave.shape, jnp.bfloat16),
            pltpu.VMEM((bonds * tiles, states, states), jnp.bfloat16),
            pltpu.VMEM((peers + 1, states, states), jnp.float32),
            pltpu.SemaphoreType.DMA((len(tables),)),
            pltpu.SemaphoreType.DMA,
            pltpu.SemaphoreType.DMA,
            pltpu.SemaphoreType.DMA,
        ],
        compiler_params=pltpu.CompilerParams(vmem_limit_bytes=40 * 1024 * 1024),
        name="couple",
    )(*in_hbm(*tables, wave, left, right))


SETS = (((1, 0), (1, 1), (3, 0)), ((2, 0), (2, 1), (3, 1)))
SHARED = (0, 1)


def pair_at(dz, dy, sign):
    n_left = lax.axis_size("lsec")
    z = lax.rem(lax.axis_index("lsec") + n_left + sign * dz, n_left)
    return z * 2 + jnp.bitwise_xor(lax.axis_index("rsec"), dy)


def pair_of(core, i, sign):
    return pair_at(*(jnp.where(core == 0, SETS[0][i][d], SETS[1][i][d]) for d in range(2)), sign)


def first_kernel(own_table, other_table, received, held, part, chosen, total):
    core = lax.rem(lax.axis_index("mpo"), 2)
    quarter = (total.shape[0] - 1) // 4
    total[...] = jnp.zeros_like(total)
    total[own_table[0, pair_at(0, 0, 1)]] = held[0].astype(jnp.float32)
    total[own_table[0, pair_at(*SHARED, -1)]] += received[0].astype(jnp.float32)
    targets = [table[0, pair_of(core, i, -1)] for i in range(3) for table in (own_table, other_table)]
    for side, half in enumerate((1 - core, core)):
        for x in range(2):
            for j in range(quarter):
                at = (side * 2 + x) * quarter + j
                tile = (2 * x + half) * quarter + j
                part[at] = total[tile]
                for s, target in enumerate(targets):
                    one = jnp.where(target == tile, 1.0, 0.0)
                    chosen[s, at] = jnp.full(chosen.shape[2:], one, jnp.float32)


def second_kernel(part, chosen, early, near, nearest, give, keep):
    slots = [early[0], early[1], near[0], near[1], nearest[0], nearest[1]]
    half, states = give.shape[0], give.shape[1]
    for at in range(2 * half):
        tile = part[at].reshape(states // 8, 8, states)
        for s, slot in enumerate(slots):
            rows = slot.astype(jnp.float32).reshape(states // 8, 8, states)
            tile += rows * chosen[s, at][None]
        tile = tile.reshape(states, states)
        if at < half:
            give[at] = tile.astype(jnp.bfloat16)
        else:
            keep[at - half] = tile


def gather(own_table, other_table, held, early, near, nearest, shared, tiles):
    states = held.shape[1]
    whole = (tiles, states, states)
    part, chosen = pl.pallas_call(
        first_kernel,
        out_shape=[
            jax.ShapeDtypeStruct(whole, jnp.float32),
            jax.ShapeDtypeStruct((6, tiles, 8, states), jnp.float32),
        ],
        in_specs=[SMEM] * 2 + [VMEM] * 2,
        out_specs=[VMEM] * 2,
        scratch_shapes=[pltpu.VMEM((tiles + 1, states, states), jnp.float32)],
        compiler_params=pltpu.CompilerParams(vmem_limit_bytes=16 * 1024 * 1024),
        name="first_sums",
        cost_estimate=pl.CostEstimate(flops=2 * 10**9, bytes_accessed=10**6, transcendentals=0),
    )(own_table, other_table, shared, held)
    return pl.pallas_call(
        second_kernel,
        out_shape=[
            jax.ShapeDtypeStruct((tiles // 2, states, states), jnp.bfloat16),
            jax.ShapeDtypeStruct((tiles // 2, states, states), jnp.float32),
        ],
        in_specs=[VMEM] * 5,
        out_specs=[VMEM] * 2,
        compiler_params=pltpu.CompilerParams(vmem_limit_bytes=16 * 1024 * 1024),
        name="second_sums",
    )(part, chosen, early, near, nearest)


def cross_kernel(received, kept, give, keep):
    half = give.shape[0]
    x = lax.axis_index("mpo") // 2
    for j in range(half):
        away, here = (1 - x) * half + j, x * half + j
        give[j] = (kept[away] + received[away].astype(jnp.float32)).astype(jnp.bfloat16)
        keep[j] = kept[here] + received[here].astype(jnp.float32)


def cross(received, kept):
    half, states = kept.shape[0] // 2, kept.shape[1]
    return pl.pallas_call(
        cross_kernel,
        out_shape=[
            jax.ShapeDtypeStruct((half, states, states), jnp.bfloat16),
            jax.ShapeDtypeStruct((half, states, states), jnp.float32),
        ],
        in_specs=[VMEM] * 2,
        out_specs=[VMEM] * 2,
        compiler_params=pltpu.CompilerParams(vmem_limit_bytes=8 * 1024 * 1024),
        name="cross",
    )(received, kept)


def by_permutes(sizes, wave, left, right, left_sizes, right_sizes, tile_left, tile_right, send_slot, recv_tile):
    n_left, n_right, n_mpo = sizes
    axes = ("lsec", "rsec", "mpo")
    place = lambda z, y, m: (z * n_right + y) * n_mpo + m
    every = [(z, y, m) for z in range(n_left) for y in range(n_right) for m in range(n_mpo)]
    swap_core = [(m, m ^ 1) for m in range(n_mpo)]
    swap_chip = [(m, m ^ 2) for m in range(n_mpo)]
    other_table = lax.ppermute(recv_tile, "mpo", swap_core)

    share = wave.shape[0] // n_mpo
    core = lambda flip: jnp.bitwise_xor(lax.rem(lax.axis_index("mpo"), 2), flip)
    give, rest, live = couple(
        [
            (lambda: [pair_of(core(1), i, 1) for i in range(3)], 3),
            (
                lambda: [pair_of(core(0), i, 1) for i in range(3)] + [pair_at(*SHARED, 1), pair_at(0, 0, 1)],
                5,
            ),
        ],
        (lambda: lax.axis_index("mpo") * share, share),
        n_left * n_right,
        tile_left, tile_right, left_sizes, right_sizes, send_slot, wave, left, right,
    )

    def move(x, steps):
        perm = [
            (place(z, y, m), place((z + steps[m % 2][0]) % n_left, y ^ steps[m % 2][1], m))
            for z, y, m in every
        ]
        return lax.ppermute(x, axes, perm)

    give, other_table = lax.optimization_barrier((give, other_table))
    got = lax.ppermute(give, "mpo", swap_core)
    keep, shared, held = rest[:3], rest[3:4], rest[4:]
    shared = move(shared, (SHARED, SHARED))
    received = [
        move(jnp.stack([keep[i], got[i]]), (SETS[0][i], SETS[1][i])) for i in range(3)
    ]
    give, keep = gather(recv_tile, other_table, held, *received, shared, wave.shape[0])
    give, keep = cross(lax.ppermute(give, "mpo", swap_core), keep)
    summed = keep + lax.ppermute(give, "mpo", swap_chip).astype(jnp.float32)
    return jnp.where(live > 0, summed, 0.0).astype(jnp.bfloat16)


def by_exchange(sizes, wave, left, right, left_sizes, right_sizes, tile_left, tile_right, send_slot, recv_tile):
    peers = sizes[0] * sizes[1]
    tiles, states = wave.shape[0], wave.shape[1]
    share = tiles // sizes[2]
    outgoing, live = couple(
        [(lambda: list(range(peers)), peers)],
        (lambda: lax.axis_index("mpo") * share, share),
        peers,
        tile_left, tile_right, left_sizes, right_sizes, send_slot, wave, left, right,
    )
    received = lax.all_to_all(outgoing, ("lsec", "rsec"), split_axis=0, concat_axis=0, tiled=True)
    chooser = (recv_tile[0][None, :] == jnp.arange(tiles, dtype=jnp.int32)[:, None]).astype(
        jnp.bfloat16
    )
    partial = jnp.dot(
        chooser, received.reshape(peers, states * states), preferred_element_type=jnp.float32
    )
    partial = partial.reshape(tiles, states, states).astype(jnp.bfloat16)
    mine = lax.psum_scatter(partial, "mpo", scatter_dimension=0, tiled=True)
    return jnp.where(live > 0, mine, jnp.zeros_like(mine))


def solution(mesh):
    sizes = tuple(mesh.shape[axis] for axis in ("lsec", "rsec", "mpo"))
    few = sizes == (4, 2, 4)
    placed = (
        P(("lsec", "rsec"), None, None),
        P("mpo", "lsec", None, None),
        P("mpo", "rsec", None, None),
        P("lsec"),
        P("rsec"),
        P(("lsec", "rsec")),
        P(("lsec", "rsec")),
        P("mpo", ("lsec", "rsec")),
        P("mpo", ("lsec", "rsec")),
    )
    return jax.shard_map(
        functools.partial(by_permutes if few else by_exchange, sizes),
        mesh=mesh,
        in_specs=placed,
        out_specs=P(("lsec", "rsec", "mpo"), None, None),
        check_vma=False,
    )
```

```python
import functools

import jax
import jax.numpy as jnp
from jax import lax
from jax.experimental import pallas as pl
from jax.experimental.pallas import tpu as pltpu
from jax.sharding import PartitionSpec as P

SMEM = pl.BlockSpec(memory_space=pltpu.SMEM)
VMEM = pl.BlockSpec(memory_space=pltpu.VMEM)
HBM = pl.BlockSpec(memory_space=pltpu.HBM)


def in_hbm(*arrays):
    return [pltpu.with_memory_space_constraint(x, pltpu.HBM) for x in arrays]


def inside(states, rows, cols):
    at_row = lax.broadcasted_iota(jnp.int32, (states, states), 0)
    at_col = lax.broadcasted_iota(jnp.int32, (states, states), 1)
    return (at_row < rows) & (at_col < cols)


def couple_kernel(groups, share, *refs):
    tables_hbm, (wave_hbm, left_hbm, right_hbm), rest = refs[:5], refs[5:8], refs[8:]
    outs, live, rest = rest[: len(groups)], rest[len(groups)], rest[len(groups) + 1 :]
    tables, rest = rest[:5], rest[5:]
    wave, left, right, masked, done, total, table_sem, wave_sem, left_sem, right_sem = rest
    tile_left, tile_right, left_sizes, right_sizes, send_slot = tables
    bonds, tiles, states = left.shape[0], wave.shape[0], wave.shape[1]
    table_copies = [
        pltpu.make_async_copy(src, dst, table_sem.at[i])
        for i, (src, dst) in enumerate(zip(tables_hbm, tables))
    ]
    for copy in table_copies:
        copy.start()
    wave_copy = pltpu.make_async_copy(wave_hbm, wave, wave_sem)
    wave_copy.start()
    right_copy = pltpu.make_async_copy(right_hbm, right, right_sem)
    right_copy.start()
    total[...] = jnp.zeros_like(total)
    for copy in table_copies:
        copy.wait()
    left_copy = pltpu.make_async_copy(left_hbm, left, left_sem)
    left_copy.start()
    for j in range(live.shape[0]):
        h = share() + j
        keep = inside(states, left_sizes[tile_left[h]], right_sizes[tile_right[h]])
        live[j] = jnp.where(keep, 1.0, 0.0).astype(jnp.bfloat16)
    wave_copy.wait()
    for g in range(tiles):
        keep = inside(states, left_sizes[tile_left[g]], right_sizes[tile_right[g]])
        tile = wave[g].astype(jnp.float32)
        masked[g] = jnp.where(keep, tile, 0.0).astype(jnp.bfloat16)
    right_copy.wait()
    for g in range(tiles):
        blocks = jnp.concatenate([right[a, tile_right[g]] for a in range(bonds)], 0)
        wide = lax.dot_general(
            masked[g], blocks, (((1,), (1,)), ((), ())), preferred_element_type=jnp.float32
        ).astype(jnp.bfloat16)
        for a in range(bonds):
            done[a * tiles + g] = wide[:, a * states : (a + 1) * states]
    left_copy.wait()
    for g in range(tiles):
        for a in range(bonds):
            total[send_slot[g, a]] += jnp.dot(
                left[a, tile_left[g]], done[a * tiles + g], preferred_element_type=jnp.float32
            )

    for out, order in zip(outs, groups):
        for j, q in enumerate(order()):
            out[j] = total[q].astype(jnp.bfloat16)


def couple(groups, share, peers, tile_left, tile_right, left_sizes, right_sizes, send_slot, wave, left, right):
    tiles, states = wave.shape[0], wave.shape[1]
    bonds = left.shape[0]
    counts = [count for _, count in groups] + [share[1]]
    tables = (tile_left, tile_right, left_sizes, right_sizes, send_slot.T)
    return pl.pallas_call(
        functools.partial(couple_kernel, [g for g, _ in groups], share[0]),
        out_shape=[jax.ShapeDtypeStruct((count, states, states), jnp.bfloat16) for count in counts],
        in_specs=[HBM] * 8,
        out_specs=[VMEM] * len(counts),
        scratch_shapes=[pltpu.SMEM(table.shape, jnp.int32) for table in tables]
        + [
            pltpu.VMEM(wave.shape, jnp.bfloat16),
            pltpu.VMEM(left.shape, jnp.bfloat16),
            pltpu.VMEM(right.shape, jnp.bfloat16),
            pltpu.VMEM(wave.shape, jnp.bfloat16),
            pltpu.VMEM((bonds * tiles, states, states), jnp.bfloat16),
            pltpu.VMEM((peers + 1, states, states), jnp.float32),
            pltpu.SemaphoreType.DMA((len(tables),)),
            pltpu.SemaphoreType.DMA,
            pltpu.SemaphoreType.DMA,
            pltpu.SemaphoreType.DMA,
        ],
        compiler_params=pltpu.CompilerParams(vmem_limit_bytes=40 * 1024 * 1024),
        name="couple",
    )(*in_hbm(*tables, wave, left, right))


SETS = (((1, 1), (0, 1), (3, 1)), ((2, 0), (2, 1), (3, 0)))
SHARED = (1, 0)


def pair_at(step, flip, sign):
    z, n_left = lax.axis_index("lsec"), lax.axis_size("lsec")
    shifted = lax.rem(z + n_left + sign * step, n_left)
    to = jnp.where(flip == 0, jnp.bitwise_xor(z, step), shifted)
    return to * 2 + jnp.bitwise_xor(lax.axis_index("rsec"), flip)


def pair_of(core, i, sign):
    return pair_at(*(jnp.where(core == 0, SETS[0][i][d], SETS[1][i][d]) for d in range(2)), sign)


def first_kernel(own_table, other_table, received, held, part, chosen, total):
    core = lax.rem(lax.axis_index("mpo"), 2)
    quarter = (total.shape[0] - 1) // 4
    total[...] = jnp.zeros_like(total)
    total[own_table[0, pair_at(0, 0, 1)]] = held[0].astype(jnp.float32)
    total[own_table[0, pair_at(*SHARED, -1)]] += received[0].astype(jnp.float32)
    targets = [table[0, pair_of(core, i, -1)] for i in range(3) for table in (own_table, other_table)]
    for side, half in enumerate((1 - core, core)):
        for x in range(2):
            for j in range(quarter):
                at = (side * 2 + x) * quarter + j
                tile = (2 * x + half) * quarter + j
                part[at] = total[tile]
                for s, target in enumerate(targets):
                    one = jnp.where(target == tile, 1.0, 0.0)
                    chosen[s, at] = jnp.full(chosen.shape[2:], one, jnp.float32)


def second_kernel(part, chosen, early, near, nearest, give, keep):
    slots = [early[0], early[1], near[0], near[1], nearest[0], nearest[1]]
    half, states = give.shape[0], give.shape[1]
    for at in range(2 * half):
        tile = part[at].reshape(states // 8, 8, states)
        for s, slot in enumerate(slots):
            rows = slot.astype(jnp.float32).reshape(states // 8, 8, states)
            tile += rows * chosen[s, at][None]
        tile = tile.reshape(states, states)
        if at < half:
            give[at] = tile.astype(jnp.bfloat16)
        else:
            keep[at - half] = tile


def gather(own_table, other_table, held, early, near, nearest, shared, tiles):
    states = held.shape[1]
    whole = (tiles, states, states)
    part, chosen = pl.pallas_call(
        first_kernel,
        out_shape=[
            jax.ShapeDtypeStruct(whole, jnp.float32),
            jax.ShapeDtypeStruct((6, tiles, 8, states), jnp.float32),
        ],
        in_specs=[SMEM] * 2 + [VMEM] * 2,
        out_specs=[VMEM] * 2,
        scratch_shapes=[pltpu.VMEM((tiles + 1, states, states), jnp.float32)],
        compiler_params=pltpu.CompilerParams(vmem_limit_bytes=16 * 1024 * 1024),
        name="first_sums",
        cost_estimate=pl.CostEstimate(flops=2 * 10**9, bytes_accessed=10**6, transcendentals=0),
    )(own_table, other_table, shared, held)
    return pl.pallas_call(
        second_kernel,
        out_shape=[
            jax.ShapeDtypeStruct((tiles // 2, states, states), jnp.bfloat16),
            jax.ShapeDtypeStruct((tiles // 2, states, states), jnp.float32),
        ],
        in_specs=[VMEM] * 5,
        out_specs=[VMEM] * 2,
        compiler_params=pltpu.CompilerParams(vmem_limit_bytes=16 * 1024 * 1024),
        name="second_sums",
    )(part, chosen, early, near, nearest)


def cross_kernel(received, kept, give, keep):
    half = give.shape[0]
    x = lax.axis_index("mpo") // 2
    for j in range(half):
        away, here = (1 - x) * half + j, x * half + j
        give[j] = (kept[away] + received[away].astype(jnp.float32)).astype(jnp.bfloat16)
        keep[j] = kept[here] + received[here].astype(jnp.float32)


def cross(received, kept):
    half, states = kept.shape[0] // 2, kept.shape[1]
    return pl.pallas_call(
        cross_kernel,
        out_shape=[
            jax.ShapeDtypeStruct((half, states, states), jnp.bfloat16),
            jax.ShapeDtypeStruct((half, states, states), jnp.float32),
        ],
        in_specs=[VMEM] * 2,
        out_specs=[VMEM] * 2,
        compiler_params=pltpu.CompilerParams(vmem_limit_bytes=8 * 1024 * 1024),
        name="cross",
    )(received, kept)


def by_permutes(sizes, wave, left, right, left_sizes, right_sizes, tile_left, tile_right, send_slot, recv_tile):
    n_left, n_right, n_mpo = sizes
    axes = ("lsec", "rsec", "mpo")
    place = lambda z, y, m: (z * n_right + y) * n_mpo + m
    every = [(z, y, m) for z in range(n_left) for y in range(n_right) for m in range(n_mpo)]
    swap_core = [(m, m ^ 1) for m in range(n_mpo)]
    swap_chip = [(m, m ^ 2) for m in range(n_mpo)]
    other_table = lax.ppermute(recv_tile, "mpo", swap_core)

    share = wave.shape[0] // n_mpo
    core = lambda flip: jnp.bitwise_xor(lax.rem(lax.axis_index("mpo"), 2), flip)
    give, rest, live = couple(
        [
            (lambda: [pair_of(core(1), i, 1) for i in range(3)], 3),
            (
                lambda: [pair_of(core(0), i, 1) for i in range(3)] + [pair_at(*SHARED, 1), pair_at(0, 0, 1)],
                5,
            ),
        ],
        (lambda: lax.axis_index("mpo") * share, share),
        n_left * n_right,
        tile_left, tile_right, left_sizes, right_sizes, send_slot, wave, left, right,
    )

    def goes(z, y, step, flip):
        return ((z + step) % n_left if flip else z ^ step), y ^ flip

    def move(x, steps):
        perm = [
            (place(z, y, m), place(*goes(z, y, *steps[m % 2]), m))
            for z, y, m in every
        ]
        return lax.ppermute(x, axes, perm)

    give, other_table = lax.optimization_barrier((give, other_table))
    got = lax.ppermute(give, "mpo", swap_core)
    keep, shared, held = rest[:3], rest[3:4], rest[4:]
    shared = move(shared, (SHARED, SHARED))
    received = [
        move(jnp.stack([keep[i], got[i]]), (SETS[0][i], SETS[1][i])) for i in range(3)
    ]
    give, keep = gather(recv_tile, other_table, held, *received, shared, wave.shape[0])
    give, keep = cross(lax.ppermute(give, "mpo", swap_core), keep)
    summed = keep + lax.ppermute(give, "mpo", swap_chip).astype(jnp.float32)
    return jnp.where(live > 0, summed, 0.0).astype(jnp.bfloat16)


def by_exchange(sizes, wave, left, right, left_sizes, right_sizes, tile_left, tile_right, send_slot, recv_tile):
    peers = sizes[0] * sizes[1]
    tiles, states = wave.shape[0], wave.shape[1]
    share = tiles // sizes[2]
    outgoing, live = couple(
        [(lambda: list(range(peers)), peers)],
        (lambda: lax.axis_index("mpo") * share, share),
        peers,
        tile_left, tile_right, left_sizes, right_sizes, send_slot, wave, left, right,
    )
    received = lax.all_to_all(outgoing, ("lsec", "rsec"), split_axis=0, concat_axis=0, tiled=True)
    chooser = (recv_tile[0][None, :] == jnp.arange(tiles, dtype=jnp.int32)[:, None]).astype(
        jnp.bfloat16
    )
    partial = jnp.dot(
        chooser, received.reshape(peers, states * states), preferred_element_type=jnp.float32
    )
    partial = partial.reshape(tiles, states, states).astype(jnp.bfloat16)
    mine = lax.psum_scatter(partial, "mpo", scatter_dimension=0, tiled=True)
    return jnp.where(live > 0, mine, jnp.zeros_like(mine))


def solution(mesh):
    sizes = tuple(mesh.shape[axis] for axis in ("lsec", "rsec", "mpo"))
    few = sizes == (4, 2, 4)
    placed = (
        P(("lsec", "rsec"), None, None),
        P("mpo", "lsec", None, None),
        P("mpo", "rsec", None, None),
        P("lsec"),
        P("rsec"),
        P(("lsec", "rsec")),
        P(("lsec", "rsec")),
        P("mpo", ("lsec", "rsec")),
        P("mpo", ("lsec", "rsec")),
    )
    return jax.shard_map(
        functools.partial(by_permutes if few else by_exchange, sizes),
        mesh=mesh,
        in_specs=placed,
        out_specs=P(("lsec", "rsec", "mpo"), None, None),
        check_vma=False,
    )
```

```python
import functools

import jax
import jax.numpy as jnp
from jax import lax
from jax.experimental import pallas as pl
from jax.experimental.pallas import tpu as pltpu
from jax.sharding import PartitionSpec as P

SMEM = pl.BlockSpec(memory_space=pltpu.SMEM)
VMEM = pl.BlockSpec(memory_space=pltpu.VMEM)
HBM = pl.BlockSpec(memory_space=pltpu.HBM)


def in_hbm(*arrays):
    return [pltpu.with_memory_space_constraint(x, pltpu.HBM) for x in arrays]


def inside(states, rows, cols):
    at_row = lax.broadcasted_iota(jnp.int32, (states, states), 0)
    at_col = lax.broadcasted_iota(jnp.int32, (states, states), 1)
    return (at_row < rows) & (at_col < cols)


def couple_kernel(groups, share, *refs):
    tables_hbm, (wave_hbm, left_hbm, right_hbm), rest = refs[:5], refs[5:8], refs[8:]
    outs, live, rest = rest[: len(groups)], rest[len(groups)], rest[len(groups) + 1 :]
    tables, rest = rest[:5], rest[5:]
    wave, left, right, masked, done, total, table_sem, wave_sem, left_sem, right_sem = rest
    tile_left, tile_right, left_sizes, right_sizes, send_slot = tables
    bonds, tiles, states = left.shape[0], wave.shape[0], wave.shape[1]
    table_copies = [
        pltpu.make_async_copy(src, dst, table_sem.at[i])
        for i, (src, dst) in enumerate(zip(tables_hbm, tables))
    ]
    for copy in table_copies:
        copy.start()
    wave_copy = pltpu.make_async_copy(wave_hbm, wave, wave_sem)
    wave_copy.start()
    right_copy = pltpu.make_async_copy(right_hbm, right, right_sem)
    right_copy.start()
    total[...] = jnp.zeros_like(total)
    for copy in table_copies:
        copy.wait()
    left_copy = pltpu.make_async_copy(left_hbm, left, left_sem)
    left_copy.start()
    for j in range(live.shape[0]):
        h = share() + j
        keep = inside(states, left_sizes[tile_left[h]], right_sizes[tile_right[h]])
        live[j] = jnp.where(keep, 1.0, 0.0).astype(jnp.bfloat16)
    wave_copy.wait()
    for g in range(tiles):
        keep = inside(states, left_sizes[tile_left[g]], right_sizes[tile_right[g]])
        tile = wave[g].astype(jnp.float32)
        masked[g] = jnp.where(keep, tile, 0.0).astype(jnp.bfloat16)
    right_copy.wait()
    for g in range(tiles):
        blocks = jnp.concatenate([right[a, tile_right[g]] for a in range(bonds)], 0)
        wide = lax.dot_general(
            masked[g], blocks, (((1,), (1,)), ((), ())), preferred_element_type=jnp.float32
        ).astype(jnp.bfloat16)
        for a in range(bonds):
            done[a * tiles + g] = wide[:, a * states : (a + 1) * states]
    left_copy.wait()
    for g in range(tiles):
        for a in range(bonds):
            total[send_slot[g, a]] += jnp.dot(
                left[a, tile_left[g]], done[a * tiles + g], preferred_element_type=jnp.float32
            )

    for out, order in zip(outs, groups):
        for j, q in enumerate(order()):
            out[j] = total[q].astype(jnp.bfloat16)


def couple(groups, share, peers, tile_left, tile_right, left_sizes, right_sizes, send_slot, wave, left, right):
    tiles, states = wave.shape[0], wave.shape[1]
    bonds = left.shape[0]
    counts = [count for _, count in groups] + [share[1]]
    tables = (tile_left, tile_right, left_sizes, right_sizes, send_slot.T)
    return pl.pallas_call(
        functools.partial(couple_kernel, [g for g, _ in groups], share[0]),
        out_shape=[jax.ShapeDtypeStruct((count, states, states), jnp.bfloat16) for count in counts],
        in_specs=[HBM] * 8,
        out_specs=[VMEM] * len(counts),
        scratch_shapes=[pltpu.SMEM(table.shape, jnp.int32) for table in tables]
        + [
            pltpu.VMEM(wave.shape, jnp.bfloat16),
            pltpu.VMEM(left.shape, jnp.bfloat16),
            pltpu.VMEM(right.shape, jnp.bfloat16),
            pltpu.VMEM(wave.shape, jnp.bfloat16),
            pltpu.VMEM((bonds * tiles, states, states), jnp.bfloat16),
            pltpu.VMEM((peers + 1, states, states), jnp.float32),
            pltpu.SemaphoreType.DMA((len(tables),)),
            pltpu.SemaphoreType.DMA,
            pltpu.SemaphoreType.DMA,
            pltpu.SemaphoreType.DMA,
        ],
        compiler_params=pltpu.CompilerParams(vmem_limit_bytes=40 * 1024 * 1024),
        name="couple",
    )(*in_hbm(*tables, wave, left, right))


SETS = (((1, 1), (0, 1), (3, 1)), ((2, 0), (2, 1), (3, 0)))
SHARED = (1, 0)


def pair_at(step, flip, sign):
    z, n_left = lax.axis_index("lsec"), lax.axis_size("lsec")
    shifted = lax.rem(z + n_left + sign * step, n_left)
    to = jnp.where(flip == 0, jnp.bitwise_xor(z, step), shifted)
    return to * 2 + jnp.bitwise_xor(lax.axis_index("rsec"), flip)


def pair_of(core, i, sign):
    return pair_at(*(jnp.where(core == 0, SETS[0][i][d], SETS[1][i][d]) for d in range(2)), sign)


def first_kernel(own_table, other_table, received, held, part, chosen, total):
    core = lax.rem(lax.axis_index("mpo"), 2)
    quarter = (total.shape[0] - 1) // 4
    total[...] = jnp.zeros_like(total)
    total[own_table[0, pair_at(0, 0, 1)]] = held[0].astype(jnp.float32)
    total[own_table[0, pair_at(*SHARED, -1)]] += received[0].astype(jnp.float32)
    targets = [table[0, pair_of(core, i, -1)] for i in range(3) for table in (own_table, other_table)]
    chip = lax.axis_index("mpo") // 2
    for side, half in enumerate((1 - core, core)):
        for here, x in enumerate((1 - chip, chip)):
            for j in range(quarter):
                at = (side * 2 + here) * quarter + j
                tile = (2 * x + half) * quarter + j
                part[at] = total[tile]
                for s, target in enumerate(targets):
                    one = jnp.where(target == tile, 1.0, 0.0)
                    chosen[s, at] = jnp.full(chosen.shape[2:], one, jnp.float32)


def second_kernel(part, chosen, early, near, nearest, *outs):
    slots = [early[0], early[1], near[0], near[1], nearest[0], nearest[1]]
    quarter, states = outs[0].shape[0], outs[0].shape[1]
    for at in range(4 * quarter):
        tile = part[at].reshape(states // 8, 8, states)
        for s, slot in enumerate(slots):
            rows = slot.astype(jnp.float32).reshape(states // 8, 8, states)
            tile += rows * chosen[s, at][None]
        out = outs[at // quarter]
        out[at % quarter] = tile.reshape(states, states).astype(out.dtype)


def gather(own_table, other_table, held, early, near, nearest, shared, tiles):
    states = held.shape[1]
    whole = (tiles, states, states)
    part, chosen = pl.pallas_call(
        first_kernel,
        out_shape=[
            jax.ShapeDtypeStruct(whole, jnp.float32),
            jax.ShapeDtypeStruct((6, tiles, 8, states), jnp.float32),
        ],
        in_specs=[SMEM] * 2 + [VMEM] * 2,
        out_specs=[VMEM] * 2,
        scratch_shapes=[pltpu.VMEM((tiles + 1, states, states), jnp.float32)],
        compiler_params=pltpu.CompilerParams(vmem_limit_bytes=16 * 1024 * 1024),
        name="first_sums",
        cost_estimate=pl.CostEstimate(flops=2 * 10**9, bytes_accessed=10**6, transcendentals=0),
    )(own_table, other_table, shared, held)
    return pl.pallas_call(
        second_kernel,
        out_shape=[
            jax.ShapeDtypeStruct((tiles // 4, states, states), kind)
            for kind in (jnp.bfloat16, jnp.bfloat16, jnp.bfloat16, jnp.float32)
        ],
        in_specs=[VMEM] * 5,
        out_specs=[VMEM] * 4,
        compiler_params=pltpu.CompilerParams(vmem_limit_bytes=16 * 1024 * 1024),
        name="second_sums",
    )(part, chosen, early, near, nearest)


def by_permutes(sizes, wave, left, right, left_sizes, right_sizes, tile_left, tile_right, send_slot, recv_tile):
    n_left, n_right, n_mpo = sizes
    axes = ("lsec", "rsec", "mpo")
    place = lambda z, y, m: (z * n_right + y) * n_mpo + m
    every = [(z, y, m) for z in range(n_left) for y in range(n_right) for m in range(n_mpo)]
    swap_core = [(m, m ^ 1) for m in range(n_mpo)]
    swap_chip = [(m, m ^ 2) for m in range(n_mpo)]
    other_table = lax.ppermute(recv_tile, "mpo", swap_core)

    share = wave.shape[0] // n_mpo
    core = lambda flip: jnp.bitwise_xor(lax.rem(lax.axis_index("mpo"), 2), flip)
    give, rest, live = couple(
        [
            (lambda: [pair_of(core(1), i, 1) for i in range(3)], 3),
            (
                lambda: [pair_of(core(0), i, 1) for i in range(3)] + [pair_at(*SHARED, 1), pair_at(0, 0, 1)],
                5,
            ),
        ],
        (lambda: lax.axis_index("mpo") * share, share),
        n_left * n_right,
        tile_left, tile_right, left_sizes, right_sizes, send_slot, wave, left, right,
    )

    def goes(z, y, step, flip):
        return ((z + step) % n_left if flip else z ^ step), y ^ flip

    def move(x, steps):
        perm = [
            (place(z, y, m), place(*goes(z, y, *steps[m % 2]), m))
            for z, y, m in every
        ]
        return lax.ppermute(x, axes, perm)

    give, other_table = lax.optimization_barrier((give, other_table))
    got = lax.ppermute(give, "mpo", swap_core)
    keep, shared, held = rest[:3], rest[3:4], rest[4:]
    shared = move(shared, (SHARED, SHARED))
    received = [
        move(jnp.stack([keep[i], got[i]]), (SETS[0][i], SETS[1][i])) for i in range(3)
    ]
    swap_both = [(m, m ^ 3) for m in range(n_mpo)]
    to_both, to_core, to_chip, summed = gather(
        recv_tile, other_table, held, *received, shared, wave.shape[0]
    )
    for send, swap in ((to_chip, swap_chip), (to_both, swap_both), (to_core, swap_core)):
        summed += lax.ppermute(send, "mpo", swap).astype(jnp.float32)
    return jnp.where(live > 0, summed, 0.0).astype(jnp.bfloat16)


def by_exchange(sizes, wave, left, right, left_sizes, right_sizes, tile_left, tile_right, send_slot, recv_tile):
    peers = sizes[0] * sizes[1]
    tiles, states = wave.shape[0], wave.shape[1]
    share = tiles // sizes[2]
    outgoing, live = couple(
        [(lambda: list(range(peers)), peers)],
        (lambda: lax.axis_index("mpo") * share, share),
        peers,
        tile_left, tile_right, left_sizes, right_sizes, send_slot, wave, left, right,
    )
    received = lax.all_to_all(outgoing, ("lsec", "rsec"), split_axis=0, concat_axis=0, tiled=True)
    chooser = (recv_tile[0][None, :] == jnp.arange(tiles, dtype=jnp.int32)[:, None]).astype(
        jnp.bfloat16
    )
    partial = jnp.dot(
        chooser, received.reshape(peers, states * states), preferred_element_type=jnp.float32
    )
    partial = partial.reshape(tiles, states, states).astype(jnp.bfloat16)
    mine = lax.psum_scatter(partial, "mpo", scatter_dimension=0, tiled=True)
    return jnp.where(live > 0, mine, jnp.zeros_like(mine))


def solution(mesh):
    sizes = tuple(mesh.shape[axis] for axis in ("lsec", "rsec", "mpo"))
    few = sizes == (4, 2, 4)
    placed = (
        P(("lsec", "rsec"), None, None),
        P("mpo", "lsec", None, None),
        P("mpo", "rsec", None, None),
        P("lsec"),
        P("rsec"),
        P(("lsec", "rsec")),
        P(("lsec", "rsec")),
        P("mpo", ("lsec", "rsec")),
        P("mpo", ("lsec", "rsec")),
    )
    return jax.shard_map(
        functools.partial(by_permutes if few else by_exchange, sizes),
        mesh=mesh,
        in_specs=placed,
        out_specs=P(("lsec", "rsec", "mpo"), None, None),
        check_vma=False,
    )
```

```python
import functools

import jax
import jax.numpy as jnp
from jax import lax
from jax.experimental import pallas as pl
from jax.experimental.pallas import tpu as pltpu
from jax.sharding import PartitionSpec as P

SMEM = pl.BlockSpec(memory_space=pltpu.SMEM)
VMEM = pl.BlockSpec(memory_space=pltpu.VMEM)
HBM = pl.BlockSpec(memory_space=pltpu.HBM)


def in_hbm(*arrays):
    return [pltpu.with_memory_space_constraint(x, pltpu.HBM) for x in arrays]


def inside(states, rows, cols):
    at_row = lax.broadcasted_iota(jnp.int32, (states, states), 0)
    at_col = lax.broadcasted_iota(jnp.int32, (states, states), 1)
    return (at_row < rows) & (at_col < cols)


def couple_kernel(groups, share, *refs):
    tables_hbm, (wave_hbm, left_hbm, right_hbm), rest = refs[:5], refs[5:8], refs[8:]
    outs, live, rest = rest[: len(groups)], rest[len(groups)], rest[len(groups) + 1 :]
    tables, rest = rest[:5], rest[5:]
    wave, left, right, masked, done, total, table_sem, wave_sem, left_sem, right_sem = rest
    tile_left, tile_right, left_sizes, right_sizes, send_slot = tables
    bonds, tiles, states = left.shape[0], wave.shape[0], wave.shape[1]
    table_copies = [
        pltpu.make_async_copy(src, dst, table_sem.at[i])
        for i, (src, dst) in enumerate(zip(tables_hbm, tables))
    ]
    for copy in table_copies:
        copy.start()
    right_copy = pltpu.make_async_copy(right_hbm, right, right_sem)
    right_copy.start()
    wave_copy = pltpu.make_async_copy(wave_hbm, wave, wave_sem)
    wave_copy.start()
    total[...] = jnp.zeros_like(total)
    for copy in table_copies:
        copy.wait()
    left_copy = pltpu.make_async_copy(left_hbm, left, left_sem)
    left_copy.start()
    for j in range(live.shape[0]):
        h = share() + j
        keep = inside(states, left_sizes[tile_left[h]], right_sizes[tile_right[h]])
        live[j] = jnp.where(keep, 1.0, 0.0).astype(jnp.bfloat16)
    wave_copy.wait()
    for g in range(tiles):
        keep = inside(states, left_sizes[tile_left[g]], right_sizes[tile_right[g]])
        tile = wave[g].astype(jnp.float32)
        masked[g] = jnp.where(keep, tile, 0.0).astype(jnp.bfloat16)
    right_copy.wait()
    for g in range(tiles):
        blocks = jnp.concatenate([right[a, tile_right[g]] for a in range(bonds)], 0)
        wide = lax.dot_general(
            masked[g], blocks, (((1,), (1,)), ((), ())), preferred_element_type=jnp.float32
        ).astype(jnp.bfloat16)
        for a in range(bonds):
            done[a * tiles + g] = wide[:, a * states : (a + 1) * states]
    left_copy.wait()
    for g in range(tiles):
        for a in range(bonds):
            total[send_slot[g, a]] += jnp.dot(
                left[a, tile_left[g]], done[a * tiles + g], preferred_element_type=jnp.float32
            )

    for out, order in zip(outs, groups):
        for j, q in enumerate(order()):
            out[j] = total[q].astype(jnp.bfloat16)


def couple(groups, share, peers, tile_left, tile_right, left_sizes, right_sizes, send_slot, wave, left, right):
    tiles, states = wave.shape[0], wave.shape[1]
    bonds = left.shape[0]
    counts = [count for _, count in groups] + [share[1]]
    tables = (tile_left, tile_right, left_sizes, right_sizes, send_slot.T)
    return pl.pallas_call(
        functools.partial(couple_kernel, [g for g, _ in groups], share[0]),
        out_shape=[jax.ShapeDtypeStruct((count, states, states), jnp.bfloat16) for count in counts],
        in_specs=[HBM] * 8,
        out_specs=[VMEM] * len(counts),
        scratch_shapes=[pltpu.SMEM(table.shape, jnp.int32) for table in tables]
        + [
            pltpu.VMEM(wave.shape, jnp.bfloat16),
            pltpu.VMEM(left.shape, jnp.bfloat16),
            pltpu.VMEM(right.shape, jnp.bfloat16),
            pltpu.VMEM(wave.shape, jnp.bfloat16),
            pltpu.VMEM((bonds * tiles, states, states), jnp.bfloat16),
            pltpu.VMEM((peers + 1, states, states), jnp.float32),
            pltpu.SemaphoreType.DMA((len(tables),)),
            pltpu.SemaphoreType.DMA,
            pltpu.SemaphoreType.DMA,
            pltpu.SemaphoreType.DMA,
        ],
        compiler_params=pltpu.CompilerParams(vmem_limit_bytes=40 * 1024 * 1024),
        name="couple",
    )(*in_hbm(*tables, wave, left, right))


SETS = (((1, 1), (0, 1), (3, 1)), ((2, 0), (2, 1), (3, 0)))
SHARED = (1, 0)


def pair_at(step, flip, sign):
    z, n_left = lax.axis_index("lsec"), lax.axis_size("lsec")
    shifted = lax.rem(z + n_left + sign * step, n_left)
    to = jnp.where(flip == 0, jnp.bitwise_xor(z, step), shifted)
    return to * 2 + jnp.bitwise_xor(lax.axis_index("rsec"), flip)


def pair_of(core, i, sign):
    return pair_at(*(jnp.where(core == 0, SETS[0][i][d], SETS[1][i][d]) for d in range(2)), sign)


def first_kernel(own_table, other_table, received, held, part, chosen, total):
    core = lax.rem(lax.axis_index("mpo"), 2)
    quarter = (total.shape[0] - 1) // 4
    total[...] = jnp.zeros_like(total)
    total[own_table[0, pair_at(0, 0, 1)]] = held[0].astype(jnp.float32)
    total[own_table[0, pair_at(*SHARED, -1)]] += received[0].astype(jnp.float32)
    targets = [table[0, pair_of(core, i, -1)] for i in range(3) for table in (own_table, other_table)]
    chip = lax.axis_index("mpo") // 2
    for side, half in enumerate((1 - core, core)):
        for here, x in enumerate((1 - chip, chip)):
            for j in range(quarter):
                at = (side * 2 + here) * quarter + j
                tile = (2 * x + half) * quarter + j
                part[at] = total[tile]
                for s, target in enumerate(targets):
                    one = jnp.where(target == tile, 1.0, 0.0)
                    chosen[s, at] = jnp.full(chosen.shape[2:], one, jnp.float32)


def second_kernel(part, chosen, early, near, nearest, *outs):
    slots = [early[0], early[1], near[0], near[1], nearest[0], nearest[1]]
    quarter, states = outs[0].shape[0], outs[0].shape[1]
    for at in range(4 * quarter):
        tile = part[at].reshape(states // 8, 8, states)
        for s, slot in enumerate(slots):
            rows = slot.astype(jnp.float32).reshape(states // 8, 8, states)
            tile += rows * chosen[s, at][None]
        out = outs[at // quarter]
        out[at % quarter] = tile.reshape(states, states).astype(out.dtype)


def gather(own_table, other_table, held, early, near, nearest, shared, tiles):
    states = held.shape[1]
    whole = (tiles, states, states)
    part, chosen = pl.pallas_call(
        first_kernel,
        out_shape=[
            jax.ShapeDtypeStruct(whole, jnp.float32),
            jax.ShapeDtypeStruct((6, tiles, 8, states), jnp.float32),
        ],
        in_specs=[SMEM] * 2 + [VMEM] * 2,
        out_specs=[VMEM] * 2,
        scratch_shapes=[pltpu.VMEM((tiles + 1, states, states), jnp.float32)],
        compiler_params=pltpu.CompilerParams(vmem_limit_bytes=16 * 1024 * 1024),
        name="first_sums",
        cost_estimate=pl.CostEstimate(flops=2 * 10**9, bytes_accessed=10**6, transcendentals=0),
    )(own_table, other_table, shared, held)
    return pl.pallas_call(
        second_kernel,
        out_shape=[
            jax.ShapeDtypeStruct((tiles // 4, states, states), kind)
            for kind in (jnp.bfloat16, jnp.bfloat16, jnp.bfloat16, jnp.float32)
        ],
        in_specs=[VMEM] * 5,
        out_specs=[VMEM] * 4,
        compiler_params=pltpu.CompilerParams(vmem_limit_bytes=16 * 1024 * 1024),
        name="second_sums",
    )(part, chosen, early, near, nearest)


def by_permutes(sizes, wave, left, right, left_sizes, right_sizes, tile_left, tile_right, send_slot, recv_tile):
    n_left, n_right, n_mpo = sizes
    axes = ("lsec", "rsec", "mpo")
    place = lambda z, y, m: (z * n_right + y) * n_mpo + m
    every = [(z, y, m) for z in range(n_left) for y in range(n_right) for m in range(n_mpo)]
    swap_core = [(m, m ^ 1) for m in range(n_mpo)]
    swap_chip = [(m, m ^ 2) for m in range(n_mpo)]
    other_table = lax.ppermute(recv_tile, "mpo", swap_core)

    share = wave.shape[0] // n_mpo
    core = lambda flip: jnp.bitwise_xor(lax.rem(lax.axis_index("mpo"), 2), flip)
    give, rest, live = couple(
        [
            (lambda: [pair_of(core(1), i, 1) for i in range(3)], 3),
            (
                lambda: [pair_of(core(0), i, 1) for i in range(3)] + [pair_at(*SHARED, 1), pair_at(0, 0, 1)],
                5,
            ),
        ],
        (lambda: lax.axis_index("mpo") * share, share),
        n_left * n_right,
        tile_left, tile_right, left_sizes, right_sizes, send_slot, wave, left, right,
    )

    def goes(z, y, step, flip):
        return ((z + step) % n_left if flip else z ^ step), y ^ flip

    def move(x, steps):
        perm = [
            (place(z, y, m), place(*goes(z, y, *steps[m % 2]), m))
            for z, y, m in every
        ]
        return lax.ppermute(x, axes, perm)

    got = lax.ppermute(give, "mpo", swap_core)
    keep, shared, held = rest[:3], rest[3:4], rest[4:]
    shared = move(shared, (SHARED, SHARED))
    received = [
        move(jnp.stack([keep[i], got[i]]), (SETS[0][i], SETS[1][i])) for i in range(3)
    ]
    swap_both = [(m, m ^ 3) for m in range(n_mpo)]
    to_both, to_core, to_chip, summed = gather(
        recv_tile, other_table, held, *received, shared, wave.shape[0]
    )
    for send, swap in ((to_chip, swap_chip), (to_both, swap_both), (to_core, swap_core)):
        summed += lax.ppermute(send, "mpo", swap).astype(jnp.float32)
    return jnp.where(live > 0, summed, 0.0).astype(jnp.bfloat16)


def by_exchange(sizes, wave, left, right, left_sizes, right_sizes, tile_left, tile_right, send_slot, recv_tile):
    peers = sizes[0] * sizes[1]
    tiles, states = wave.shape[0], wave.shape[1]
    share = tiles // sizes[2]
    outgoing, live = couple(
        [(lambda: list(range(peers)), peers)],
        (lambda: lax.axis_index("mpo") * share, share),
        peers,
        tile_left, tile_right, left_sizes, right_sizes, send_slot, wave, left, right,
    )
    received = lax.all_to_all(outgoing, ("lsec", "rsec"), split_axis=0, concat_axis=0, tiled=True)
    chooser = (recv_tile[0][None, :] == jnp.arange(tiles, dtype=jnp.int32)[:, None]).astype(
        jnp.bfloat16
    )
    partial = jnp.dot(
        chooser, received.reshape(peers, states * states), preferred_element_type=jnp.float32
    )
    partial = partial.reshape(tiles, states, states).astype(jnp.bfloat16)
    mine = lax.psum_scatter(partial, "mpo", scatter_dimension=0, tiled=True)
    return jnp.where(live > 0, mine, jnp.zeros_like(mine))


def solution(mesh):
    sizes = tuple(mesh.shape[axis] for axis in ("lsec", "rsec", "mpo"))
    few = sizes == (4, 2, 4)
    placed = (
        P(("lsec", "rsec"), None, None),
        P("mpo", "lsec", None, None),
        P("mpo", "rsec", None, None),
        P("lsec"),
        P("rsec"),
        P(("lsec", "rsec")),
        P(("lsec", "rsec")),
        P("mpo", ("lsec", "rsec")),
        P("mpo", ("lsec", "rsec")),
    )
    return jax.shard_map(
        functools.partial(by_permutes if few else by_exchange, sizes),
        mesh=mesh,
        in_specs=placed,
        out_specs=P(("lsec", "rsec", "mpo"), None, None),
        check_vma=False,
    )
```

```python
import functools

import jax
import jax.numpy as jnp
from jax import lax
from jax.experimental import pallas as pl
from jax.experimental.pallas import tpu as pltpu
from jax.sharding import PartitionSpec as P

SMEM = pl.BlockSpec(memory_space=pltpu.SMEM)
VMEM = pl.BlockSpec(memory_space=pltpu.VMEM)
HBM = pl.BlockSpec(memory_space=pltpu.HBM)


def in_hbm(*arrays):
    return [pltpu.with_memory_space_constraint(x, pltpu.HBM) for x in arrays]


def inside(states, rows, cols):
    at_row = lax.broadcasted_iota(jnp.int32, (states, states), 0)
    at_col = lax.broadcasted_iota(jnp.int32, (states, states), 1)
    return (at_row < rows) & (at_col < cols)


def couple_kernel(groups, share, *refs):
    tables_hbm, (wave_hbm, left_hbm, right_hbm), rest = refs[:5], refs[5:8], refs[8:]
    outs, live, rest = rest[: len(groups)], rest[len(groups)], rest[len(groups) + 1 :]
    tables, rest = rest[:5], rest[5:]
    wave, left, right, masked, done, total, table_sem, wave_sem, left_sem, right_sem = rest
    tile_left, tile_right, left_sizes, right_sizes, send_slot = tables
    bonds, tiles, states = left.shape[0], wave.shape[0], wave.shape[1]
    table_copies = [
        pltpu.make_async_copy(src, dst, table_sem.at[i])
        for i, (src, dst) in enumerate(zip(tables_hbm, tables))
    ]
    for copy in table_copies:
        copy.start()
    wave_copy = pltpu.make_async_copy(wave_hbm, wave, wave_sem)
    wave_copy.start()
    right_copy = pltpu.make_async_copy(right_hbm, right, right_sem)
    right_copy.start()
    total[...] = jnp.zeros_like(total)
    for copy in table_copies:
        copy.wait()
    left_copy = pltpu.make_async_copy(left_hbm, left, left_sem)
    left_copy.start()
    for j in range(live.shape[0]):
        h = share() + j
        keep = inside(states, left_sizes[tile_left[h]], right_sizes[tile_right[h]])
        live[j] = jnp.where(keep, 1.0, 0.0).astype(jnp.bfloat16)
    wave_copy.wait()
    for g in range(tiles):
        keep = inside(states, left_sizes[tile_left[g]], right_sizes[tile_right[g]])
        tile = wave[g].astype(jnp.float32)
        masked[g] = jnp.where(keep, tile, 0.0).astype(jnp.bfloat16)
    right_copy.wait()
    for g in range(tiles):
        blocks = jnp.concatenate([right[a, tile_right[g]] for a in range(bonds)], 0)
        wide = lax.dot_general(
            masked[g], blocks, (((1,), (1,)), ((), ())), preferred_element_type=jnp.float32
        ).astype(jnp.bfloat16)
        for a in range(bonds):
            done[a * tiles + g] = wide[:, a * states : (a + 1) * states]
    left_copy.wait()
    for g in range(tiles):
        for a in range(bonds):
            total[send_slot[g, a]] += jnp.dot(
                left[a, tile_left[g]], done[a * tiles + g], preferred_element_type=jnp.float32
            )

    for out, order in zip(outs, groups):
        for j, q in enumerate(order()):
            out[j] = total[q].astype(jnp.bfloat16)


def couple(groups, share, peers, tile_left, tile_right, left_sizes, right_sizes, send_slot, wave, left, right):
    tiles, states = wave.shape[0], wave.shape[1]
    bonds = left.shape[0]
    counts = [count for _, count in groups] + [share[1]]
    tables = (tile_left, tile_right, left_sizes, right_sizes, send_slot.T)
    return pl.pallas_call(
        functools.partial(couple_kernel, [g for g, _ in groups], share[0]),
        out_shape=[jax.ShapeDtypeStruct((count, states, states), jnp.bfloat16) for count in counts],
        in_specs=[HBM] * 8,
        out_specs=[VMEM] * len(counts),
        scratch_shapes=[pltpu.SMEM(table.shape, jnp.int32) for table in tables]
        + [
            pltpu.VMEM(wave.shape, jnp.bfloat16),
            pltpu.VMEM(left.shape, jnp.bfloat16),
            pltpu.VMEM(right.shape, jnp.bfloat16),
            pltpu.VMEM(wave.shape, jnp.bfloat16),
            pltpu.VMEM((bonds * tiles, states, states), jnp.bfloat16),
            pltpu.VMEM((peers + 1, states, states), jnp.float32),
            pltpu.SemaphoreType.DMA((len(tables),)),
            pltpu.SemaphoreType.DMA,
            pltpu.SemaphoreType.DMA,
            pltpu.SemaphoreType.DMA,
        ],
        compiler_params=pltpu.CompilerParams(vmem_limit_bytes=40 * 1024 * 1024),
        name="couple",
    )(*in_hbm(*tables, wave, left, right))


SETS = (((1, 1), (0, 1), (3, 1)), ((2, 1), (2, 0), (3, 0)))
SHARED = (1, 0)


def pair_at(step, flip, sign):
    z, n_left = lax.axis_index("lsec"), lax.axis_size("lsec")
    shifted = lax.rem(z + n_left + sign * step, n_left)
    to = jnp.where(flip == 0, jnp.bitwise_xor(z, step), shifted)
    return to * 2 + jnp.bitwise_xor(lax.axis_index("rsec"), flip)


def pair_of(core, i, sign):
    return pair_at(*(jnp.where(core == 0, SETS[0][i][d], SETS[1][i][d]) for d in range(2)), sign)


def first_kernel(own_table, other_table, received, held, part, chosen, total):
    core = lax.rem(lax.axis_index("mpo"), 2)
    quarter = (total.shape[0] - 1) // 4
    total[...] = jnp.zeros_like(total)
    total[own_table[0, pair_at(0, 0, 1)]] = held[0].astype(jnp.float32)
    total[own_table[0, pair_at(*SHARED, -1)]] += received[0].astype(jnp.float32)
    targets = [table[0, pair_of(core, i, -1)] for i in range(3) for table in (own_table, other_table)]
    chip = lax.axis_index("mpo") // 2
    for side, half in enumerate((1 - core, core)):
        for here, x in enumerate((1 - chip, chip)):
            for j in range(quarter):
                at = (side * 2 + here) * quarter + j
                tile = (2 * x + half) * quarter + j
                part[at] = total[tile]
                for s, target in enumerate(targets):
                    one = jnp.where(target == tile, 1.0, 0.0)
                    chosen[s, at] = jnp.full(chosen.shape[2:], one, jnp.float32)


def second_kernel(part, chosen, early, near, nearest, *outs):
    slots = [early[0], early[1], near[0], near[1], nearest[0], nearest[1]]
    quarter, states = outs[0].shape[0], outs[0].shape[1]
    for at in range(4 * quarter):
        tile = part[at].reshape(states // 8, 8, states)
        for s, slot in enumerate(slots):
            rows = slot.astype(jnp.float32).reshape(states // 8, 8, states)
            tile += rows * chosen[s, at][None]
        out = outs[at // quarter]
        out[at % quarter] = tile.reshape(states, states).astype(out.dtype)


def gather(own_table, other_table, held, early, near, nearest, shared, tiles):
    states = held.shape[1]
    whole = (tiles, states, states)
    part, chosen = pl.pallas_call(
        first_kernel,
        out_shape=[
            jax.ShapeDtypeStruct(whole, jnp.float32),
            jax.ShapeDtypeStruct((6, tiles, 8, states), jnp.float32),
        ],
        in_specs=[SMEM] * 2 + [VMEM] * 2,
        out_specs=[VMEM] * 2,
        scratch_shapes=[pltpu.VMEM((tiles + 1, states, states), jnp.float32)],
        compiler_params=pltpu.CompilerParams(vmem_limit_bytes=16 * 1024 * 1024),
        name="first_sums",
        cost_estimate=pl.CostEstimate(flops=2 * 10**9, bytes_accessed=10**6, transcendentals=0),
    )(own_table, other_table, shared, held)
    return pl.pallas_call(
        second_kernel,
        out_shape=[
            jax.ShapeDtypeStruct((tiles // 4, states, states), kind)
            for kind in (jnp.bfloat16, jnp.bfloat16, jnp.bfloat16, jnp.float32)
        ],
        in_specs=[VMEM] * 5,
        out_specs=[VMEM] * 4,
        compiler_params=pltpu.CompilerParams(vmem_limit_bytes=16 * 1024 * 1024),
        name="second_sums",
    )(part, chosen, early, near, nearest)


def by_permutes(sizes, wave, left, right, left_sizes, right_sizes, tile_left, tile_right, send_slot, recv_tile):
    n_left, n_right, n_mpo = sizes
    axes = ("lsec", "rsec", "mpo")
    place = lambda z, y, m: (z * n_right + y) * n_mpo + m
    every = [(z, y, m) for z in range(n_left) for y in range(n_right) for m in range(n_mpo)]
    swap_core = [(m, m ^ 1) for m in range(n_mpo)]
    swap_chip = [(m, m ^ 2) for m in range(n_mpo)]
    other_table = lax.ppermute(recv_tile, "mpo", swap_core)

    share = wave.shape[0] // n_mpo
    core = lambda flip: jnp.bitwise_xor(lax.rem(lax.axis_index("mpo"), 2), flip)
    give, rest, live = couple(
        [
            (lambda: [pair_of(core(1), i, 1) for i in range(3)], 3),
            (
                lambda: [pair_of(core(0), i, 1) for i in range(3)] + [pair_at(*SHARED, 1), pair_at(0, 0, 1)],
                5,
            ),
        ],
        (lambda: lax.axis_index("mpo") * share, share),
        n_left * n_right,
        tile_left, tile_right, left_sizes, right_sizes, send_slot, wave, left, right,
    )

    def goes(z, y, step, flip):
        return ((z + step) % n_left if flip else z ^ step), y ^ flip

    def move(x, steps):
        perm = [
            (place(z, y, m), place(*goes(z, y, *steps[m % 2]), m))
            for z, y, m in every
        ]
        return lax.ppermute(x, axes, perm)

    give, other_table = lax.optimization_barrier((give, other_table))
    got = lax.ppermute(give, "mpo", swap_core)
    keep, shared, held = rest[:3], rest[3:4], rest[4:]
    shared = move(shared, (SHARED, SHARED))
    received = [
        move(jnp.stack([keep[i], got[i]]), (SETS[0][i], SETS[1][i])) for i in range(3)
    ]
    swap_both = [(m, m ^ 3) for m in range(n_mpo)]
    to_both, to_core, to_chip, summed = gather(
        recv_tile, other_table, held, *received, shared, wave.shape[0]
    )
    for send, swap in ((to_chip, swap_chip), (to_both, swap_both), (to_core, swap_core)):
        summed += lax.ppermute(send, "mpo", swap).astype(jnp.float32)
    return jnp.where(live > 0, summed, 0.0).astype(jnp.bfloat16)


def by_exchange(sizes, wave, left, right, left_sizes, right_sizes, tile_left, tile_right, send_slot, recv_tile):
    peers = sizes[0] * sizes[1]
    tiles, states = wave.shape[0], wave.shape[1]
    share = tiles // sizes[2]
    outgoing, live = couple(
        [(lambda: list(range(peers)), peers)],
        (lambda: lax.axis_index("mpo") * share, share),
        peers,
        tile_left, tile_right, left_sizes, right_sizes, send_slot, wave, left, right,
    )
    received = lax.all_to_all(outgoing, ("lsec", "rsec"), split_axis=0, concat_axis=0, tiled=True)
    chooser = (recv_tile[0][None, :] == jnp.arange(tiles, dtype=jnp.int32)[:, None]).astype(
        jnp.bfloat16
    )
    partial = jnp.dot(
        chooser, received.reshape(peers, states * states), preferred_element_type=jnp.float32
    )
    partial = partial.reshape(tiles, states, states).astype(jnp.bfloat16)
    mine = lax.psum_scatter(partial, "mpo", scatter_dimension=0, tiled=True)
    return jnp.where(live > 0, mine, jnp.zeros_like(mine))


def solution(mesh):
    sizes = tuple(mesh.shape[axis] for axis in ("lsec", "rsec", "mpo"))
    few = sizes == (4, 2, 4)
    placed = (
        P(("lsec", "rsec"), None, None),
        P("mpo", "lsec", None, None),
        P("mpo", "rsec", None, None),
        P("lsec"),
        P("rsec"),
        P(("lsec", "rsec")),
        P(("lsec", "rsec")),
        P("mpo", ("lsec", "rsec")),
        P("mpo", ("lsec", "rsec")),
    )
    return jax.shard_map(
        functools.partial(by_permutes if few else by_exchange, sizes),
        mesh=mesh,
        in_specs=placed,
        out_specs=P(("lsec", "rsec", "mpo"), None, None),
        check_vma=False,
    )
```
